512 devices in a mesh: seq: 16 (over z_lo, core), chan: 32 (over z_hi, y, x).
Axes of the slice: x: 4, y: 4, z: 16 (z_hi: 2, z_lo: 8; z = z_hi * 8 + z_lo), core: 2. Of those that a mesh axis runs over, the one named last changes fastest.
Arguments:
- features: bfloat16 [3, 16384, 8192], P(None, ('seq', 'chan')), may hold values from -6 to 6
- short_weights: float32 [3, 3, 8192], replicated, may hold values from -3.5 to 3.5
- doc_lengths: int32 [64], replicated, may hold values from 1 to 2048, 16384 in all
- residues: float32 [16, 8192], P(None, 'chan'), may hold values from -1.5 to 1.5
- rates: float32 [16, 8192], P(None, 'chan'), may hold values from 3.0517578e-05 to 0.05
- skip: float32 [8192], P('chan'), may hold values from -4 to 4
Outputs:
- mixed: bfloat16 [16384, 8192], P(('seq', 'chan'))
The draws below stay inside these ranges and needn't reach their ends.
Inputs may be any that keep to these rules, and one draw needn't show every extreme that they name: `doc_lengths`: the lengths sum to 16384 and the largest is exactly 2048.
All inputs are finite; a program needn't handle non-finite values.
Results may differ from the reference program's by a relative error of at most 0.01.
Values may be sent and summed in bfloat16 or wider, within the bound.
A program may use at most 64 MiB of HBM per device.

```python
import math
import jax
import jax.numpy as jnp
import numpy as np
from jax import lax

D = 8192
MODES = 16
TAPS = 3
NDOCS = 64
LENGTH = 16384


def steps_of(rng, shape, split, low, largest):
    def one(dim, shards_of):
        heights = jax.random.uniform(jax.random.fold_in(jax.random.fold_in(rng, 6), dim), (shards_of,), jnp.float32, low / len(split), largest / len(split))
        return jnp.repeat(jnp.exp(heights), shape[dim] // shards_of).reshape((-1,) + (1,) * (len(shape) - dim - 1))

    level = one(*split[0])
    for cut in split[1:]:
        level = level * one(*cut)
    return level


def split_up(count, total, most, lean):
    portions = [(1 << 20) // math.isqrt(rank ** lean) + 1 for rank in range(2, count + 1)]
    spare, given = total - most - (count - 1), [1] * (count - 1)
    while spare > 0:
        free = [i for i in range(count - 1) if given[i] < most]
        whole, remaining = sum([portions[i] for i in free]), spare
        for i in free:
            extra = min(most - given[i], max(1, remaining * portions[i] // whole), spare)
            given[i] = given[i] + extra
            spare = spare - extra
    return np.array([most] + given)


def uneven(key, number_of, total, most, slope):
    if number_of == 2:
        one = jax.random.randint(key, (), max(1, total - most), min(most, total - 1) + 1)
        return jnp.stack([one, total - one])
    tallies = jnp.asarray(split_up(number_of, total, most, slope), jnp.int32)
    couples = (number_of - 1) // 2
    donor, sink = tallies[1:1 + 2 * couples:2], tallies[2:2 + 2 * couples:2]
    margin = jnp.minimum(donor - 1, most - sink)
    moved = jax.random.randint(jax.random.fold_in(key, 1), (couples,), 0, 1 << 20) % (margin + 1)
    tallies = tallies.at[1:1 + 2 * couples:2].set(donor - moved).at[2:2 + 2 * couples:2].set(sink + moved)
    return tallies[jax.random.permutation(jax.random.fold_in(key, 2), number_of)]


def bell_draw(key, extent, scale, bound, cuts=(), kind=jnp.bfloat16):
    loudness = steps_of(key, extent, cuts, -0.22, 0.18) if cuts else 1.0
    result = jax.random.normal(key, extent, jnp.float32) * scale * loudness
    return jnp.minimum(jnp.maximum(result, -bound), bound).astype(kind)


def setup_inputs(seed: int = 0) -> dict:
    key_of = jax.random.split(jax.random.key(seed), 7)
    features = bell_draw(key_of[0], (3, LENGTH, D), 1.0, 6.0, ((1, 512),))
    short_weights = bell_draw(key_of[1], (3, TAPS, D), TAPS ** -0.5, 3.5, (), jnp.float32)
    doc_lengths = uneven(key_of[2], NDOCS, LENGTH, LENGTH // 8, 2).astype(jnp.int32)
    residues = bell_draw(key_of[3], (MODES, D), 0.25, 1.5, ((1, 32),), jnp.float32)
    rates = jnp.clip(jnp.exp(math.log(0.05) - 7.4014754 * jax.random.uniform(key_of[4], (MODES, D), jnp.float32) ** steps_of(key_of[4], (MODES, D), ((1, 32),), -0.2, 0.2)), 3.0517578125e-05, 0.05)
    skip = bell_draw(key_of[5], (D,), 1.0, 4.0, ((0, 32),), jnp.float32)
    return dict(features=features, short_weights=short_weights, doc_lengths=doc_lengths, residues=residues, rates=rates, skip=skip)


def spectrum_of(freq, residues, rates, length):
    total = 2 * length
    half = freq.astype(jnp.float32) * (math.pi / total)
    sine = jnp.sin(half)[:, None]
    cosine = jnp.cos(half)[:, None]
    parity = (1 - 2 * (freq % 2)).astype(jnp.float32)[:, None]
    spec_re = jnp.zeros((freq.shape[0], rates.shape[1]), jnp.float32)
    spec_im = jnp.zeros((freq.shape[0], rates.shape[1]), jnp.float32)
    for mode in range(rates.shape[0]):
        rate = rates[mode][None, :]
        residue = residues[mode][None, :]
        decay = jnp.exp(-rate)
        gap = -jnp.expm1(-rate)
        gain = residue * jnp.sqrt(-jnp.expm1(-2.0 * rate))
        tail = jnp.exp(-rate * length)
        numer = 1.0 - parity * tail
        den_re = gap + 2.0 * decay * sine * sine
        den_im = 2.0 * decay * sine * cosine
        scale = gain * numer / (den_re * den_re + den_im * den_im)
        spec_re = spec_re + scale * den_re
        spec_im = spec_im - scale * den_im
    return (spec_re, spec_im)

def reference(features, short_weights, doc_lengths, residues, rates, skip):
    length = LENGTH
    width = D
    cols = min(width, 512)
    position = jnp.arange(length, dtype=jnp.int32)
    starts = (jnp.cumsum(doc_lengths) - doc_lengths).astype(jnp.int32)
    begin = lax.optimization_barrier(jnp.max(jnp.where(starts[None, :] <= position[:, None], starts[None, :], 0), axis=1)).astype(jnp.int32)
    freq = jnp.arange(length + 1, dtype=jnp.int32)

    def one_block(index):
        start = index * cols
        values = lax.dynamic_slice_in_dim(features, start, cols, 2).astype(jnp.float32)
        weights = lax.dynamic_slice_in_dim(short_weights, start, cols, 2)
        streams = jnp.zeros(values.shape, jnp.float32)
        for offset in range(TAPS):
            valid = (position - offset >= begin).astype(jnp.float32)
            moved = jnp.pad(values, ((0, 0), (offset, 0), (0, 0)))[:, :length, :]
            streams = streams + valid[None, :, None] * weights[:, offset, None, :] * moved
        gate = streams[0].astype(jnp.bfloat16)
        product = (streams[1] * streams[2]).astype(jnp.bfloat16)
        part_res = lax.dynamic_slice_in_dim(residues, start, cols, 1)
        part_rate = lax.dynamic_slice_in_dim(rates, start, cols, 1)
        spec_re, spec_im = spectrum_of(freq, part_res, part_rate, length)
        spectrum = jnp.fft.rfft(product.astype(jnp.float32), n=2 * length, axis=0)
        conv = jnp.fft.irfft(spectrum * lax.complex(spec_re, spec_im), n=2 * length, axis=0)[:length]
        part_skip = lax.dynamic_slice_in_dim(skip, start, cols, 0)
        mixed = gate.astype(jnp.float32) * (conv + part_skip[None, :] * product.astype(jnp.float32))
        return mixed.astype(jnp.bfloat16)
    blocks = lax.map(one_block, jnp.arange(width // cols, dtype=jnp.int32))
    return jnp.transpose(blocks, (1, 0, 2)).reshape(length, width)
```

```python
import functools

import jax
import jax.numpy as jnp
from jax import lax
from jax.experimental import pallas as pl
from jax.experimental.pallas import tpu as pltpu
from jax.sharding import PartitionSpec as P

MODES = 16
LANES = 128
QUADS = 4
HALF = 256
VMEM = pl.BlockSpec(memory_space=pltpu.VMEM)
PARAMS = pltpu.CompilerParams(vmem_limit_bytes=48 * 2**20)


def doc_starts(doc_ref):
    n = doc_ref.shape[1]
    lengths = doc_ref[...].astype(jnp.float32)
    rows = lax.broadcasted_iota(jnp.int32, (n, n), 0)
    cols = lax.broadcasted_iota(jnp.int32, (n, n), 1)
    wide = jnp.broadcast_to(lengths, (n, n))
    column = jnp.sum(jnp.where(rows == cols, wide, 0.0), axis=1, keepdims=True)
    return jnp.sum(jnp.where(rows < cols, column, 0.0), axis=0, keepdims=True)


def featurize(first, doc_ref, feat_ref, rim_ref, short_ref, gate_ref, prod_ref):
    rows = feat_ref.shape[1]
    peers = prod_ref.shape[0]
    starts = doc_starts(doc_ref)
    n = starts.shape[1]
    index = lax.broadcasted_iota(jnp.int32, (rows, n), 0)
    position = (first + index).astype(jnp.float32)
    here = jnp.max(jnp.where(starts == position, 1.0, 0.0), axis=1, keepdims=True)
    before = jnp.max(jnp.where(starts == position - 1.0, 1.0, 0.0), axis=1, keepdims=True)
    one = jnp.broadcast_to(here, (rows, HALF)) < 0.5
    two = jnp.broadcast_to(here + before, (rows, HALF)) < 0.5
    row = lax.broadcasted_iota(jnp.int32, (rows, HALF), 0)

    @pl.loop(0, 2 * peers)
    def _(block):
        cols = pl.ds(pl.multiple_of(block * HALF, HALF), HALF)
        streams = []
        for s in range(3):
            x = feat_ref[s, :, cols].astype(jnp.float32)
            rim = rim_ref[s, :, cols].astype(jnp.float32)
            x1 = jnp.where(row == 0, rim[1:2], pltpu.roll(x, 1, 0))
            x2 = jnp.where(row == 0, rim[0:1], jnp.where(row == 1, rim[1:2], pltpu.roll(x, 2, 0)))
            streams.append(
                x * short_ref[s, 0:1, cols]
                + jnp.where(one, x1, 0.0) * short_ref[s, 1:2, cols]
                + jnp.where(two, x2, 0.0) * short_ref[s, 2:3, cols]
            )
        gate_ref[:, cols] = streams[0].astype(jnp.bfloat16)
        value = (streams[1] * streams[2]).astype(jnp.bfloat16)

        @pl.when(block < peers)
        def _():
            prod_ref[block, :, 0:HALF] = value

        @pl.when(block >= peers)
        def _():
            prod_ref[block - peers, :, HALF : 2 * HALF] = value


def scatter_params(modes_ref, rate_ref, gain_ref, skip_ref):
    for q in range(QUADS):
        cols = slice((q % 2) * LANES, (q % 2 + 1) * LANES)
        rate = modes_ref[q // 2, 0:MODES, cols]
        gain = modes_ref[q // 2, MODES : 2 * MODES, cols]
        skip = modes_ref[q // 2, 2 * MODES : 2 * MODES + 1, cols]
        for h in range(2):
            at = h * QUADS + q
            rate_ref[pl.ds(at, MODES, stride=8), :] = rate
            gain_ref[pl.ds(at, MODES, stride=8), :] = gain
            skip_ref[at : at + 1, :] = skip


def spread(recv_ref, u_ref):
    peers, rows, _ = recv_ref.shape
    steps = peers * rows // 2

    @pl.loop(0, peers)
    def _(p):
        h = p // (peers // 2)
        t = (p % (peers // 2)) * rows
        for q in range(QUADS):
            at = pl.multiple_of((h * QUADS + q) * steps + t, 32)
            u_ref[pl.ds(at, rows), :] = recv_ref[p, :, q * LANES : (q + 1) * LANES].astype(jnp.float32)


def mode_rows(ref):
    return [ref[m * 8 : m * 8 + 8, :] for m in range(MODES)]


def local_states(u_ref, rate_ref, end_ref, steps):
    decay = [jnp.exp(-x) for x in mode_rows(rate_ref)]

    def step(t, x):
        u = u_ref[pl.ds(t, 8, stride=steps), :]
        return tuple(d * a + u for d, a in zip(decay, x))

    zero = jnp.zeros((8, LANES), jnp.float32)
    x = lax.fori_loop(0, steps, step, (zero,) * MODES, unroll=8)
    for m in range(MODES):
        end_ref[m * 8 : m * 8 + 8, :] = x[m]


def block_states(end_ref, rate_ref, state_ref, steps):
    for m in range(MODES):
        x = end_ref[m * 8 : m * 8 + 8, :]
        rate = rate_ref[m * 8 : m * 8 + 4, :]
        state_ref[m * 4 : m * 4 + 4, :] = jnp.exp(-float(steps) * rate) * x[0:4] + x[4:8]


def local_outputs(u_ref, rate_ref, gain_ref, skip_ref, y_ref, steps):
    decay = [jnp.exp(-x) for x in mode_rows(rate_ref)]
    gain = mode_rows(gain_ref)
    skip = skip_ref[...]

    def step(t, x):
        u = u_ref[pl.ds(t, 8, stride=steps), :]
        x = tuple(d * a + u for d, a in zip(decay, x))
        parts = [g * a for g, a in zip(gain, x)] + [skip * u]
        while len(parts) > 1:
            parts = [sum(parts[i : i + 2]) for i in range(0, len(parts), 2)]
        y_ref[pl.ds(t, 8, stride=steps), :] = parts[0]
        return x

    zero = jnp.zeros((8, LANES), jnp.float32)
    lax.fori_loop(0, steps, step, (zero,) * MODES, unroll=4)


def carried(end_ref, carry_ref, rate_ref, gain_ref, steps):
    out = []
    for m in range(MODES):
        carry = carry_ref[m * 4 : m * 4 + 4, :]
        rate = rate_ref[m * 8 : m * 8 + 4, :]
        later = end_ref[m * 8 : m * 8 + 4, :] + jnp.exp(-float(steps) * rate) * carry
        out.append(gain_ref[m * 8 : m * 8 + 8, :] * jnp.concatenate([carry, later], axis=0))
    return tuple(out)


def add_carried(state, decay, y_ref, t, steps):
    state = tuple(d * a for d, a in zip(decay, state))
    parts = list(state)
    while len(parts) > 1:
        parts = [sum(parts[i : i + 2]) for i in range(0, len(parts), 2)]
    rows = pl.ds(t, 8, stride=steps)
    y_ref[rows, :] = y_ref[rows, :] + parts[0]
    return state


def gathered(y_ref, out_ref, p, h, t, rows, steps):
    for q in range(QUADS):
        at = pl.multiple_of((h * QUADS + q) * steps + t, 32)
        out_ref[p, :, q * LANES : (q + 1) * LANES] = y_ref[pl.ds(at, rows), :].astype(jnp.bfloat16)


def featurize_kernel(doc_ref, feat_ref, rim_ref, short_ref, gate_ref, prod_ref):
    me = lax.axis_index("seq") * lax.axis_size("chan") + lax.axis_index("chan")
    featurize(me * feat_ref.shape[1], doc_ref, feat_ref, rim_ref, short_ref, gate_ref, prod_ref)


def filter_kernel(recv_ref, modes_ref, state_ref, end_ref, y_ref, u_ref, rate_ref, gain_ref, skip_ref):
    steps = recv_ref.shape[0] * recv_ref.shape[1] // 2
    scatter_params(modes_ref, rate_ref, gain_ref, skip_ref)
    spread(recv_ref, u_ref)
    local_states(u_ref, rate_ref, end_ref, steps)
    block_states(end_ref, rate_ref, state_ref, steps)
    local_outputs(u_ref, rate_ref, gain_ref, skip_ref, y_ref, steps)


def finish_kernel(all_ref, end_ref, yin_ref, modes_ref, out_ref, y_ref, rate_ref, gain_ref, skip_ref, carry_ref):
    peers, rows, _ = out_ref.shape
    steps = peers * rows // 2
    scatter_params(modes_ref, rate_ref, gain_ref, skip_ref)
    me = lax.axis_index("seq") * 2 + lax.axis_index("chan") // peers
    decay = [jnp.exp(-2.0 * steps * rate_ref[m * 8 : m * 8 + 4, :]) for m in range(MODES)]

    def earlier(b, x):
        s = all_ref[b]
        return tuple(
            jnp.where(b < me, d * a + s[m * 4 : m * 4 + 4, :], a)
            for m, (d, a) in enumerate(zip(decay, x))
        )

    zero = jnp.zeros((QUADS, LANES), jnp.float32)
    x = lax.fori_loop(0, all_ref.shape[0], earlier, (zero,) * MODES)
    for m in range(MODES):
        carry_ref[m * 4 : m * 4 + 4, :] = x[m]
    y_ref[...] = yin_ref[...]
    state = carried(end_ref, carry_ref, rate_ref, gain_ref, steps)
    decay = [jnp.exp(-x) for x in mode_rows(rate_ref)]

    def part(i, state):
        state = lax.fori_loop(
            0, rows, lambda t, s: add_carried(s, decay, y_ref, i * rows + t, steps), state, unroll=8
        )
        for h in range(2):
            gathered(y_ref, out_ref, h * (peers // 2) + i, h, i * rows, rows, steps)
        return state

    lax.fori_loop(0, peers // 2, part, state)


def per_device(features, short_weights, doc_lengths, residues, rates, skip):
    seqs = lax.axis_size("seq")
    chans = lax.axis_size("chan")
    peers = chans // 2
    blocks = 2 * seqs
    rows, width = features.shape[1:]
    steps = peers * rows // 2
    bf16, f32 = jnp.bfloat16, jnp.float32
    sds = jax.ShapeDtypeStruct
    chan = lax.axis_index("chan")

    count = seqs * chans
    rim = lax.ppermute(
        features[:, rows - 2 :, :], ("seq", "chan"), [(i, (i + 1) % count) for i in range(count)]
    )
    gains = residues * jnp.sqrt(-jnp.expm1(-2.0 * rates))
    mine = jnp.concatenate([rates, gains, jnp.pad(skip[None, :], ((0, 7), (0, 0)))])
    other = lax.ppermute(mine, "chan", [(i, (i + peers) % chans) for i in range(chans)])
    modes = jnp.where(chan < peers, jnp.stack([mine, other]), jnp.stack([other, mine]))

    gate, product = pl.pallas_call(
        featurize_kernel,
        out_shape=(sds((rows, width), bf16), sds((peers, rows, 2 * HALF), bf16)),
        in_specs=[VMEM] * 4,
        out_specs=(VMEM, VMEM),
        compiler_params=PARAMS,
    )(doc_lengths[None, :], features, rim, short_weights)
    plane = [[z * peers + p for p in range(peers)] for z in range(2)]
    received = lax.all_to_all(product, "chan", 0, 0, axis_index_groups=plane, tiled=True)
    wide = (2 * QUADS * steps, LANES)
    table = pltpu.VMEM((8 * MODES, LANES), f32)
    state, end, local = pl.pallas_call(
        filter_kernel,
        out_shape=(sds((MODES * QUADS, LANES), f32), sds((8 * MODES, LANES), f32), sds(wide, f32)),
        in_specs=[VMEM] * 2,
        out_specs=(VMEM,) * 3,
        scratch_shapes=[pltpu.VMEM(wide, f32), table, table, pltpu.VMEM((8, LANES), f32)],
        compiler_params=PARAMS,
    )(received, modes)
    column = [
        [s * chans + z * peers + p for s in range(seqs) for z in range(2)] for p in range(peers)
    ]
    states = lax.all_gather(state, ("seq", "chan"), axis_index_groups=column)
    mixed = pl.pallas_call(
        finish_kernel,
        out_shape=sds((peers, rows, 2 * HALF), bf16),
        in_specs=[VMEM] * 4,
        out_specs=VMEM,
        scratch_shapes=[
            pltpu.VMEM(wide, f32),
            table,
            table,
            pltpu.VMEM((8, LANES), f32),
            pltpu.VMEM((MODES * QUADS, LANES), f32),
        ],
        compiler_params=PARAMS,
    )(states, end, local, modes)
    back = lax.all_to_all(mixed, "chan", 0, 0, axis_index_groups=plane, tiled=True)
    back = back.reshape(peers, rows, 2, HALF).transpose(1, 2, 0, 3).reshape(rows, width)
    return (gate.astype(f32) * back.astype(f32)).astype(bf16)


def solution(mesh):
    placed = (P(None, ("seq", "chan"), None), P(), P(), P(None, "chan"), P(None, "chan"), P("chan"))
    return jax.shard_map(
        per_device, mesh=mesh, in_specs=placed, out_specs=P(("seq", "chan"), None), check_vma=False
    )
```

```python
import jax
import jax.numpy as jnp
from jax import lax
from jax.experimental import pallas as pl
from jax.experimental.pallas import tpu as pltpu
from jax.sharding import PartitionSpec as P

MODES = 16
LANES = 128
QUADS = 4
HALF = 256
VMEM = pl.BlockSpec(memory_space=pltpu.VMEM)
MESH = pl.DeviceIdType.MESH


def doc_starts(doc_ref):
    n = doc_ref.shape[1]
    lengths = doc_ref[...].astype(jnp.float32)
    rows = lax.broadcasted_iota(jnp.int32, (n, n), 0)
    cols = lax.broadcasted_iota(jnp.int32, (n, n), 1)
    wide = jnp.broadcast_to(lengths, (n, n))
    column = jnp.sum(jnp.where(rows == cols, wide, 0.0), axis=1, keepdims=True)
    return jnp.sum(jnp.where(rows < cols, column, 0.0), axis=0, keepdims=True)


def tap_masks(first, doc_ref, rows):
    starts = doc_starts(doc_ref)
    n = starts.shape[1]
    index = lax.broadcasted_iota(jnp.int32, (rows, n), 0)
    position = (first + index).astype(jnp.float32)
    here = jnp.max(jnp.where(starts == position, 1.0, 0.0), axis=1, keepdims=True)
    before = jnp.max(jnp.where(starts == position - 1.0, 1.0, 0.0), axis=1, keepdims=True)
    one = jnp.broadcast_to(here, (rows, HALF)) < 0.5
    two = jnp.broadcast_to(here + before, (rows, HALF)) < 0.5
    return one, two


def featurize(block, one, two, feat_ref, rim_ref, short_ref, gate_ref):
    row = lax.broadcasted_iota(jnp.int32, one.shape, 0)
    cols = pl.ds(pl.multiple_of(block * HALF, HALF), HALF)
    streams = []
    for s in range(3):
        x = feat_ref[s, :, cols].astype(jnp.float32)
        rim = rim_ref[s, :, cols].astype(jnp.float32)
        x1 = jnp.where(row == 0, rim[1:2], pltpu.roll(x, 1, 0))
        x2 = jnp.where(row == 0, rim[0:1], jnp.where(row == 1, rim[1:2], pltpu.roll(x, 2, 0)))
        streams.append(
            x * short_ref[s, 0:1, cols]
            + jnp.where(one, x1, 0.0) * short_ref[s, 1:2, cols]
            + jnp.where(two, x2, 0.0) * short_ref[s, 2:3, cols]
        )
    gate_ref[:, cols] = streams[0].astype(jnp.bfloat16)
    return (streams[1] * streams[2]).astype(jnp.bfloat16)


def mode_gain(rate, residue):
    x = 2.0 * rate
    series = jnp.ones_like(x)
    for n in range(9, 1, -1):
        series = 1.0 - x * (1.0 / n) * series
    return residue * jnp.sqrt(x * series)


def scatter_params(modes_ref, rate_ref, gain_ref, skip_ref):
    for q in range(QUADS):
        cols = slice((q % 2) * LANES, (q % 2 + 1) * LANES)
        rate = modes_ref[q // 2, 0:MODES, cols]
        gain = modes_ref[q // 2, MODES : 2 * MODES, cols]
        skip = modes_ref[q // 2, 2 * MODES : 2 * MODES + 1, cols]
        for h in range(2):
            at = h * QUADS + q
            rate_ref[pl.ds(at, MODES, stride=8), :] = rate
            gain_ref[pl.ds(at, MODES, stride=8), :] = gain
            skip_ref[at : at + 1, :] = skip


def spread(p, recv_ref, u_ref):
    peers, rows, _ = recv_ref.shape
    steps = peers * rows // 2
    h = p // (peers // 2)
    t = (p % (peers // 2)) * rows
    for q in range(QUADS):
        at = pl.multiple_of((h * QUADS + q) * steps + t, 32)
        u_ref[pl.ds(at, rows), :] = recv_ref[p, :, q * LANES : (q + 1) * LANES].astype(jnp.float32)


def mode_rows(ref):
    return [ref[m * 8 : m * 8 + 8, :] for m in range(MODES)]


def local_states(u_ref, rate_ref, end_ref, steps):
    decay = [jnp.exp(-x) for x in mode_rows(rate_ref)]

    def step(t, x):
        u = u_ref[pl.ds(t, 8, stride=steps), :]
        return tuple(d * a + u for d, a in zip(decay, x))

    zero = jnp.zeros((8, LANES), jnp.float32)
    x = lax.fori_loop(0, steps, step, (zero,) * MODES, unroll=8)
    for m in range(MODES):
        end_ref[m * 8 : m * 8 + 8, :] = x[m]


def block_states(end_ref, rate_ref, state_ref, steps):
    height = state_ref.shape[1]
    for m in range(MODES):
        x = end_ref[m * 8 : m * 8 + 8, :]
        rate = rate_ref[m * 8 : m * 8 + 4, :]
        state = jnp.exp(-float(steps) * rate) * x[0:4] + x[4:8]
        put_rows(state_ref, m, state)


def put_rows(ref, m, value):
    height = ref.shape[1]
    if height <= QUADS:
        for i in range(QUADS // height):
            ref[m * (QUADS // height) + i] = value[i * height : (i + 1) * height]
    else:
        each = height // QUADS
        ref[m // each, (m % each) * QUADS : (m % each + 1) * QUADS, :] = value


def get_rows(ref, m):
    height = ref.shape[1]
    if height <= QUADS:
        n = QUADS // height
        return jnp.concatenate([ref[m * n + i] for i in range(n)], axis=0)
    each = height // QUADS
    return ref[m // each, (m % each) * QUADS : (m % each + 1) * QUADS, :]


def local_outputs(x, begin, end, u_ref, rate_ref, gain_ref, skip_ref, y_ref, steps):
    decay = [jnp.exp(-x) for x in mode_rows(rate_ref)]
    gain = mode_rows(gain_ref)
    skip = skip_ref[...]

    def step(t, x):
        u = u_ref[pl.ds(t, 8, stride=steps), :]
        x = tuple(d * a + u for d, a in zip(decay, x))
        y_ref[pl.ds(t, 8, stride=steps), :] = total([g * a for g, a in zip(gain, x)] + [skip * u])
        return x

    return lax.fori_loop(begin, end, step, x, unroll=4)


def total(parts):
    while len(parts) > 1:
        parts = [sum(parts[i : i + 2]) for i in range(0, len(parts), 2)]
    return parts[0]


def carried(end_ref, carry_ref, rate_ref, gain_ref, base_ref, steps):
    for m in range(MODES):
        carry = get_rows(carry_ref, m)
        rate = rate_ref[m * 8 : m * 8 + 4, :]
        later = end_ref[m * 8 : m * 8 + 4, :] + jnp.exp(-float(steps) * rate) * carry
        both = jnp.concatenate([carry, later], axis=0)
        base_ref[m * 8 : m * 8 + 8, :] = gain_ref[m * 8 : m * 8 + 8, :] * both


def add_carried(i, rows, base_ref, rate_ref, y_ref, steps):
    rate = mode_rows(rate_ref)
    decay = [jnp.exp(-x) for x in rate]
    begin = i * rows
    past = begin.astype(jnp.float32)
    state = tuple(a * jnp.exp(-past * r) for a, r in zip(mode_rows(base_ref), rate))

    def step(t, state):
        state = tuple(d * a for d, a in zip(decay, state))
        at = pl.ds(begin + t, 8, stride=steps)
        y_ref[at, :] = y_ref[at, :] + total(list(state))
        return state

    lax.fori_loop(0, rows, step, state, unroll=8)


def gathered(y_ref, out_ref, p, h, t, rows, steps):
    for q in range(QUADS):
        at = pl.multiple_of((h * QUADS + q) * steps + t, 32)
        out_ref[p, :, q * LANES : (q + 1) * LANES] = y_ref[pl.ds(at, rows), :].astype(jnp.bfloat16)


def kernel(
    doc_ref, feat_ref, short_ref, residues_ref, rates_ref, skipin_ref,
    out_ref,
    rim_ref, rimin_ref, modes_ref, gate_ref, prod_ref, recv_ref, u_ref, y_ref, mixed_ref, back_ref,
    rate_ref, gain_ref, skip_ref, end_ref, base_ref, state_ref, states_ref, carries_ref, carry_ref, fade_ref,
    pair_send, pair_recv, there_send, there_recv, back_send, back_recv, ring_send, ring_recv,
):
    seqs, chans = lax.axis_size("seq"), lax.axis_size("chan")
    seq, chan = lax.axis_index("seq"), lax.axis_index("chan")
    peers, rows, _ = prod_ref.shape
    blocks = 2 * seqs
    steps = peers * rows // 2
    z, plane = chan // peers, chan % peers
    block = seq * 2 + z
    me = seq * chans + chan
    count = seqs * chans
    after, prior = (me + 1) % count, (me + count - 1) % count

    def in_plane(p):
        return (seq, z * peers + p)

    def in_column(b):
        return (b // 2, (b % 2) * peers + plane)

    def of_all(i):
        return (i // chans, i % chans)

    barrier = pltpu.get_barrier_semaphore()

    def greet(device):
        pl.semaphore_signal(barrier, inc=1, device_id=device, device_id_type=MESH)

    greet(of_all(prior))

    @pl.loop(1, peers)
    def _(k):
        greet(in_plane((plane + k) % peers))

    @pl.loop(1, blocks)
    def _(k):
        greet(in_column((block + k) % blocks))

    for s in range(3):
        rim_ref[s] = feat_ref[s, rows - 2 : rows, :]
    rates = rates_ref[...]
    modes_ref[z, 0:MODES, :] = rates
    modes_ref[z, MODES : 2 * MODES, :] = mode_gain(rates, residues_ref[...])
    modes_ref[z, 2 * MODES : 2 * MODES + 8, :] = jnp.broadcast_to(skipin_ref[...], (8, HALF))
    one, two = tap_masks(me * rows, doc_ref, rows)

    pl.semaphore_wait(barrier, peers + blocks - 1)

    rim = pltpu.make_async_remote_copy(
        rim_ref, rimin_ref, pair_send.at[0], pair_recv.at[0], device_id=of_all(after), device_id_type=MESH
    )
    rim.start()

    def params(slot):
        return pltpu.make_async_remote_copy(
            modes_ref.at[slot], modes_ref.at[slot], pair_send.at[1], pair_recv.at[1],
            device_id=in_plane_of_other(), device_id_type=MESH,
        )

    def in_plane_of_other():
        return (seq, (1 - z) * peers + plane)

    params(z).start()
    rim.wait_recv()

    def there(p, slot):
        return pltpu.make_async_remote_copy(
            prod_ref.at[p], recv_ref.at[slot], there_send.at[p], there_recv.at[slot],
            device_id=in_plane(p), device_id_type=MESH,
        )

    def make(p):
        for half in range(2):
            value = featurize(half * peers + p, one, two, feat_ref, rimin_ref, short_ref, gate_ref)
            prod_ref[p, :, half * HALF : (half + 1) * HALF] = value

    @pl.loop(1, peers)
    def _(k):
        p = (plane + k) % peers
        make(p)
        there(p, plane).start()

    make(plane)
    recv_ref[plane] = prod_ref[plane]
    spread(plane, recv_ref, u_ref)
    params(1 - z).wait_recv()
    scatter_params(modes_ref, rate_ref, gain_ref, skip_ref)
    for m in range(MODES):
        put_rows(fade_ref, m, jnp.exp(-2.0 * steps * rate_ref[m * 8 : m * 8 + 4, :]))

    @pl.loop(1, peers)
    def _(k):
        p = (plane + peers - k) % peers
        there(plane, p).wait_recv()
        spread(p, recv_ref, u_ref)

    local_states(u_ref, rate_ref, end_ref, steps)
    block_states(end_ref, rate_ref, state_ref, steps)

    def state_copy(b, slot):
        return pltpu.make_async_remote_copy(
            state_ref.at[b], states_ref.at[slot], ring_send.at[b], ring_recv.at[slot],
            device_id=in_column(b), device_id_type=MESH,
        )

    def carry_copy(b, slot):
        return pltpu.make_async_remote_copy(
            carries_ref.at[b], carry_ref.at[slot], ring_send.at[blocks + b], ring_recv.at[blocks + slot],
            device_id=in_column(b), device_id_type=MESH,
        )

    @pl.loop(1, blocks)
    def _(k):
        state_copy((block + k) % blocks, block).start()

    states_ref[block] = state_ref[block]

    zero = (jnp.zeros((8, LANES), jnp.float32),) * MODES
    x = local_outputs(zero, 0, steps // 2, u_ref, rate_ref, gain_ref, skip_ref, y_ref, steps)

    @pl.loop(1, blocks)
    def _(k):
        state_copy(block, (block + k) % blocks).wait_recv()

    fade = fade_ref[block]

    def chain(b, carry):
        carries_ref[b] = carry
        return fade * carry + states_ref[b]

    lax.fori_loop(0, blocks, chain, jnp.zeros_like(fade))

    @pl.loop(1, blocks)
    def _(k):
        carry_copy((block + k) % blocks, block).start()

    carry_ref[block] = carries_ref[block]
    local_outputs(x, steps // 2, steps, u_ref, rate_ref, gain_ref, skip_ref, y_ref, steps)

    @pl.loop(1, blocks)
    def _(k):
        carry_copy(block, (block + k) % blocks).wait_recv()

    carried(end_ref, carry_ref, rate_ref, gain_ref, base_ref, steps)

    def back(p, slot):
        return pltpu.make_async_remote_copy(
            mixed_ref.at[p], back_ref.at[slot], back_send.at[p], back_recv.at[slot],
            device_id=in_plane(p), device_id_type=MESH,
        )

    @pl.loop(0, peers // 2)
    def _(k):
        i = (plane + k) % (peers // 2)
        add_carried(i, rows, base_ref, rate_ref, y_ref, steps)
        for h in range(2):
            p = h * (peers // 2) + i
            gathered(y_ref, mixed_ref, p, h, i * rows, rows, steps)

            @pl.when(p != plane)
            def _():
                back(p, plane).start()

    back_ref[plane] = mixed_ref[plane]

    def finish(p):
        for half in range(2):
            cols = pl.ds(pl.multiple_of((half * peers + p) * HALF, HALF), HALF)
            value = back_ref[p, :, half * HALF : (half + 1) * HALF].astype(jnp.float32)
            out_ref[:, cols] = (gate_ref[:, cols].astype(jnp.float32) * value).astype(jnp.bfloat16)

    finish(plane)

    @pl.loop(1, peers)
    def _(k):
        p = (plane + k) % peers
        back(plane, p).wait_recv()
        finish(p)

    rim.wait_send()
    params(z).wait_send()

    @pl.loop(1, peers)
    def _(k):
        p = (plane + k) % peers
        there(p, plane).wait_send()
        back(p, plane).wait_send()

    @pl.loop(1, blocks)
    def _(k):
        b = (block + k) % blocks
        state_copy(b, block).wait_send()
        carry_copy(b, block).wait_send()


def per_device(features, short_weights, doc_lengths, residues, rates, skip):
    blocks = 2 * lax.axis_size("seq")
    peers = lax.axis_size("chan") // 2
    rows, width = features.shape[1:]
    wide = pltpu.VMEM((peers * rows * QUADS, LANES), jnp.float32)
    table = pltpu.VMEM((8 * MODES, LANES), jnp.float32)
    rim = pltpu.VMEM((3, 2, width), jnp.bfloat16)
    moved = pltpu.VMEM((peers, rows, 2 * HALF), jnp.bfloat16)
    slices = pltpu.VMEM((blocks, MODES * QUADS // blocks, LANES), jnp.float32)
    dma = pltpu.SemaphoreType.DMA
    return pl.pallas_call(
        kernel,
        out_shape=jax.ShapeDtypeStruct((rows, width), jnp.bfloat16),
        in_specs=[VMEM] * 6,
        out_specs=VMEM,
        scratch_shapes=[
            rim, rim,
            pltpu.VMEM((2, 2 * MODES + 8, HALF), jnp.float32),
            pltpu.VMEM((rows, width), jnp.bfloat16),
            moved, moved, wide, wide, moved, moved,
            table, table, pltpu.VMEM((8, LANES), jnp.float32), table, table,
            slices, slices, slices, slices, slices,
            dma((2,)), dma((2,)), dma((peers,)), dma((peers,)), dma((peers,)), dma((peers,)),
            dma((2 * blocks,)), dma((2 * blocks,)),
        ],
        compiler_params=pltpu.CompilerParams(
            collective_id=0, has_side_effects=True, vmem_limit_bytes=40 * 2**20
        ),
    )(doc_lengths[None, :], features, short_weights, residues, rates, skip[None, :])


def solution(mesh):
    placed = (P(None, ("seq", "chan"), None), P(), P(), P(None, "chan"), P(None, "chan"), P("chan"))
    return jax.shard_map(
        per_device, mesh=mesh, in_specs=placed, out_specs=P(("seq", "chan"), None), check_vma=False
    )
```

```python
import jax
import jax.numpy as jnp
from jax import lax
from jax.experimental import pallas as pl
from jax.experimental.pallas import tpu as pltpu
from jax.sharding import PartitionSpec as P

MODES = 16
LANES = 128
QUADS = 4
HALF = 256
VMEM = pl.BlockSpec(memory_space=pltpu.VMEM)
MESH = pl.DeviceIdType.MESH


def doc_starts(doc_ref):
    n = doc_ref.shape[1]
    lengths = doc_ref[...].astype(jnp.float32)
    rows = lax.broadcasted_iota(jnp.int32, (n, n), 0)
    cols = lax.broadcasted_iota(jnp.int32, (n, n), 1)
    wide = jnp.broadcast_to(lengths, (n, n))
    column = jnp.sum(jnp.where(rows == cols, wide, 0.0), axis=1, keepdims=True)
    return jnp.sum(jnp.where(rows < cols, column, 0.0), axis=0, keepdims=True)


def tap_masks(first, doc_ref, rows):
    starts = doc_starts(doc_ref)
    n = starts.shape[1]
    index = lax.broadcasted_iota(jnp.int32, (rows, n), 0)
    position = (first + index).astype(jnp.float32)
    here = jnp.max(jnp.where(starts == position, 1.0, 0.0), axis=1, keepdims=True)
    before = jnp.max(jnp.where(starts == position - 1.0, 1.0, 0.0), axis=1, keepdims=True)
    one = jnp.broadcast_to(here, (rows, HALF)) < 0.5
    two = jnp.broadcast_to(here + before, (rows, HALF)) < 0.5
    return one, two


def filtered(x, x1, x2, one, two, short_ref, s, cols):
    return (
        x * short_ref[s, 0:1, cols]
        + jnp.where(one, x1, 0.0) * short_ref[s, 1:2, cols]
        + jnp.where(two, x2, 0.0) * short_ref[s, 2:3, cols]
    )


def form_product(block, one, two, feat_ref, short_ref):
    rows = one.shape[0]
    cols = pl.ds(pl.multiple_of(block * HALF, HALF), HALF)
    streams, ends = [], []
    for s in (1, 2):
        x = feat_ref[s, :, cols].astype(jnp.float32)
        ends.append((x[0:8], x[rows - 8 : rows]))
        streams.append(
            filtered(x, pltpu.roll(x, 1, 0), pltpu.roll(x, 2, 0), one, two, short_ref, s, cols)
        )
    row = lax.broadcasted_iota(jnp.int32, (8, HALF), 0)
    (key_top, key_end), (value_top, value_end) = ends
    lower = jnp.where(row < 6, pltpu.roll(value_end, 6, 0), key_end)
    upper = jnp.where(row < 2, key_top, pltpu.roll(value_top, 2, 0))
    edges = jnp.where(row < 4, upper, lower)
    return (streams[0] * streams[1]).astype(jnp.bfloat16), edges.astype(jnp.bfloat16)


def form_gate(block, one, two, feat_ref, rim_ref, short_ref, gate_ref):
    row = lax.broadcasted_iota(jnp.int32, one.shape, 0)
    cols = pl.ds(pl.multiple_of(block * HALF, HALF), HALF)
    x = feat_ref[0, :, cols].astype(jnp.float32)
    rim = rim_ref[:, cols].astype(jnp.float32)
    x1 = jnp.where(row == 0, rim[1:2], pltpu.roll(x, 1, 0))
    x2 = jnp.where(row == 0, rim[0:1], jnp.where(row == 1, rim[1:2], pltpu.roll(x, 2, 0)))
    gate_ref[:, cols] = filtered(x, x1, x2, one, two, short_ref, 0, cols).astype(jnp.bfloat16)


def repair(first, rows, plane, doc_ref, short_ref, edge_ref, u_ref):
    peers = edge_ref.shape[0] // (8 * QUADS) - 1
    steps = peers * rows // 2
    starts = doc_starts(doc_ref)
    n = starts.shape[1]
    index = lax.broadcasted_iota(jnp.int32, (peers, n), 0)
    position = (first + index * rows).astype(jnp.float32)

    def begins(shift):
        hit = jnp.where(starts == position + shift, 1.0, 0.0)
        return jnp.broadcast_to(jnp.max(hit, axis=1, keepdims=True), (peers, HALF))

    before, here, later = begins(-1.0), begins(0.0), begins(1.0)
    one = (here < 0.5, later < 0.5)
    two = (here + before < 0.5, later + here < 0.5)
    for half in range(2):
        cols = pl.ds(pl.multiple_of((half * peers + plane) * HALF, HALF), HALF)
        lanes = slice(half * HALF, (half + 1) * HALF)

        def edge(slot, r):
            parts = [
                edge_ref[pl.ds((half * 2 + i) * 8 * (peers + 1) + slot * 8 + r, peers, stride=8), :]
                for i in range(HALF // LANES)
            ]
            return jnp.concatenate(parts, axis=1)

        fixed = []
        for s, top, last in ((1, 0, 6), (2, 2, 4)):
            x = [edge(0, last), edge(0, last + 1), edge(1, top), edge(1, top + 1)]
            fixed.append(
                [
                    filtered(x[2 + i], x[1 + i], x[i], one[i], two[i], short_ref, s, cols)
                    for i in range(2)
                ]
            )
        for i in range(2):
            value = (fixed[0][i] * fixed[1][i]).astype(jnp.bfloat16).astype(jnp.float32)
            for h in range(2):
                for j in range(HALF // LANES):
                    q = half * (HALF // LANES) + j
                    at = pl.ds((h * QUADS + q) * steps + i, peers // 2, stride=rows)
                    u_ref[at, :] = value[h * (peers // 2) : (h + 1) * (peers // 2), j * LANES : (j + 1) * LANES]


def mode_gain(rate, residue):
    x = 2.0 * rate
    series = jnp.ones_like(x)
    for n in range(9, 1, -1):
        series = 1.0 - x * (1.0 / n) * series
    return residue * jnp.sqrt(x * series)


def scatter_rates(modes_ref, rate_ref):
    for q in range(QUADS):
        cols = slice((q % 2) * LANES, (q % 2 + 1) * LANES)
        for h in range(2):
            rate_ref[pl.ds(h * QUADS + q, MODES, stride=8), :] = modes_ref[q // 2, 0:MODES, cols]


def scatter_gains(modes_ref, gain_ref, skip_ref):
    for q in range(QUADS):
        cols = slice((q % 2) * LANES, (q % 2 + 1) * LANES)
        for h in range(2):
            at = h * QUADS + q
            gain_ref[pl.ds(at, MODES, stride=8), :] = modes_ref[q // 2, MODES : 2 * MODES, cols]
            skip_ref[at : at + 1, :] = modes_ref[q // 2, 2 * MODES : 2 * MODES + 1, cols]


def spread(p, recv_ref, u_ref):
    peers, rows, _ = recv_ref.shape
    steps = peers * rows // 2
    h = p // (peers // 2)
    t = (p % (peers // 2)) * rows
    for q in range(QUADS):
        at = pl.multiple_of((h * QUADS + q) * steps + t, 32)
        u_ref[pl.ds(at, rows), :] = recv_ref[p, :, q * LANES : (q + 1) * LANES].astype(jnp.float32)


def mode_rows(ref):
    return [ref[m * 8 : m * 8 + 8, :] for m in range(MODES)]


def local_states(u_ref, rate_ref, end_ref, steps):
    decay = [jnp.exp(-x) for x in mode_rows(rate_ref)]

    def step(t, x):
        u = u_ref[pl.ds(t, 8, stride=steps), :]
        return tuple(d * a + u for d, a in zip(decay, x))

    zero = jnp.zeros((8, LANES), jnp.float32)
    x = lax.fori_loop(0, steps, step, (zero,) * MODES, unroll=8)
    for m in range(MODES):
        end_ref[m * 8 : m * 8 + 8, :] = x[m]


def block_states(end_ref, rate_ref, state_ref, steps):
    for m in range(MODES):
        x = end_ref[m * 8 : m * 8 + 8, :]
        rate = rate_ref[m * 8 : m * 8 + 4, :]
        state = jnp.exp(-float(steps) * rate) * x[0:4] + x[4:8]
        put_rows(state_ref, m, state)


def put_rows(ref, m, value):
    height = ref.shape[1]
    if height <= QUADS:
        for i in range(QUADS // height):
            ref[m * (QUADS // height) + i] = value[i * height : (i + 1) * height]
    else:
        each = height // QUADS
        ref[m // each, (m % each) * QUADS : (m % each + 1) * QUADS, :] = value


def get_rows(ref, m):
    height = ref.shape[1]
    if height <= QUADS:
        n = QUADS // height
        return jnp.concatenate([ref[m * n + i] for i in range(n)], axis=0)
    each = height // QUADS
    return ref[m // each, (m % each) * QUADS : (m % each + 1) * QUADS, :]


def local_outputs(x, begin, end, u_ref, rate_ref, gain_ref, skip_ref, y_ref, steps):
    decay = [jnp.exp(-x) for x in mode_rows(rate_ref)]
    gain = mode_rows(gain_ref)
    skip = skip_ref[...]

    def step(t, x):
        u = u_ref[pl.ds(t, 8, stride=steps), :]
        x = tuple(d * a + u for d, a in zip(decay, x))
        y_ref[pl.ds(t, 8, stride=steps), :] = total([g * a for g, a in zip(gain, x)] + [skip * u])
        return x

    return lax.fori_loop(begin, end, step, x, unroll=4)


def total(parts):
    while len(parts) > 1:
        parts = [sum(parts[i : i + 2]) for i in range(0, len(parts), 2)]
    return parts[0]


def carried(end_ref, carry_ref, rate_ref, gain_ref, base_ref, steps):
    for m in range(MODES):
        carry = get_rows(carry_ref, m)
        rate = rate_ref[m * 8 : m * 8 + 4, :]
        later = end_ref[m * 8 : m * 8 + 4, :] + jnp.exp(-float(steps) * rate) * carry
        both = jnp.concatenate([carry, later], axis=0)
        base_ref[m * 8 : m * 8 + 8, :] = gain_ref[m * 8 : m * 8 + 8, :] * both


def add_carried(i, rows, base_ref, rate_ref, y_ref, steps):
    rate = mode_rows(rate_ref)
    decay = [jnp.exp(-x) for x in rate]
    begin = i * rows
    past = begin.astype(jnp.float32)
    state = tuple(a * jnp.exp(-past * r) for a, r in zip(mode_rows(base_ref), rate))

    def step(t, state):
        state = tuple(d * a for d, a in zip(decay, state))
        at = pl.ds(begin + t, 8, stride=steps)
        y_ref[at, :] = y_ref[at, :] + total(list(state))
        return state

    lax.fori_loop(0, rows, step, state, unroll=8)


def gathered(y_ref, out_ref, p, h, t, rows, steps):
    for q in range(QUADS):
        at = pl.multiple_of((h * QUADS + q) * steps + t, 32)
        out_ref[p, :, q * LANES : (q + 1) * LANES] = y_ref[pl.ds(at, rows), :].astype(jnp.bfloat16)


def kernel(
    doc_hbm, feat_hbm, short_hbm, residues_hbm, rates_hbm, skip_hbm,
    out_ref,
    doc_ref, feat_ref, short_ref, residues_ref, rates_ref, skipin_ref,
    rim_ref, rimin_ref, modes_ref, gate_ref, prod_ref, recv_ref, edge_ref, edges_ref, cross_ref, edgewide_ref,
    u_ref, y_ref, mixed_ref, back_ref,
    rate_ref, gain_ref, skip_ref, end_ref, base_ref, state_ref, packed_ref, states_ref, carries_ref, carry_ref, fade_ref,
    load, pair_send, pair_recv, cross_send, there_send, there_recv, edge_send, edge_recv, back_send, back_recv,
    ring_send, ring_recv, near_send, near_recv,
):
    seqs, chans = lax.axis_size("seq"), lax.axis_size("chan")
    seq, chan = lax.axis_index("seq"), lax.axis_index("chan")
    peers, rows, _ = prod_ref.shape
    blocks = 2 * seqs
    owners = state_ref.shape[0]
    steps = peers * rows // 2
    z, plane = chan // peers, chan % peers
    block = seq * 2 + z
    me = seq * chans + chan
    count = seqs * chans
    after, prior = (me + 1) % count, (me + count - 1) % count

    def in_plane(p):
        return (seq, z * peers + p)

    def in_column(b):
        return (b // 2, (b % 2) * peers + plane)

    def of_all(i):
        return (i // chans, i % chans)

    def remote(src, dst, send, recv, device):
        return pltpu.make_async_remote_copy(src, dst, send, recv, device_id=device, device_id_type=MESH)

    barrier = pltpu.get_barrier_semaphore()

    def greet(device):
        pl.semaphore_signal(barrier, inc=1, device_id=device, device_id_type=MESH)

    @pl.loop(1, blocks)
    def _(k):
        greet(in_column((block + k) % blocks))

    behind = (block + blocks - 1) % blocks
    greet((behind // 2, (behind % 2) * peers + peers - 1))
    greet(of_all(prior))

    @pl.loop(1, peers)
    def _(k):
        greet(in_plane((plane + k) % peers))

    pairs = (
        (feat_hbm, feat_ref), (short_hbm, short_ref), (doc_hbm, doc_ref), (rates_hbm, rates_ref),
        (residues_hbm, residues_ref), (skip_hbm, skipin_ref),
    )
    loads = [pltpu.make_async_copy(src, dst, load.at[i]) for i, (src, dst) in enumerate(pairs)]
    for copy in loads:
        copy.start()
    for copy in loads[2:]:
        copy.wait()
    rates = rates_ref[...]
    modes_ref[z, 0:MODES, :] = rates
    modes_ref[z, MODES : 2 * MODES, :] = mode_gain(rates, residues_ref[...])
    modes_ref[z, 2 * MODES : 2 * MODES + 8, :] = jnp.broadcast_to(skipin_ref[...], (8, HALF))
    one, two = tap_masks(me * rows, doc_ref, rows)
    for copy in loads[:2]:
        copy.wait()
    rim_ref[...] = feat_ref[0, rows - 2 : rows, :]

    @pl.loop(0, peers)
    def _(p):
        for half in range(2):
            value, edges = form_product(half * peers + p, one, two, feat_ref, short_ref)
            prod_ref[p, :, half * HALF : (half + 1) * HALF] = value
            edge_ref[p, :, half * HALF : (half + 1) * HALF] = edges

    pl.semaphore_wait(barrier, peers + blocks - 1 + peers * (plane // (peers - 1)))

    partner = (seq, (1 - z) * peers + plane)

    def params(slot, part):
        at = modes_ref.at[slot, pl.ds(0, MODES)] if part == 0 else modes_ref.at[slot, pl.ds(MODES, MODES + 8)]
        return remote(at, at, pair_send.at[part], pair_recv.at[part], partner)

    params(z, 0).start()

    def cross(p):
        ahead = (block + 1) % blocks
        return remote(
            edge_ref.at[p], cross_ref, cross_send.at[p], pair_recv.at[3],
            (ahead // 2, (ahead % 2) * peers + p),
        )

    @pl.when(plane == peers - 1)
    def _():
        @pl.loop(0, peers)
        def _(p):
            cross(p).start()

    def edges_there(p, slot):
        return remote(edge_ref.at[p], edges_ref.at[slot], edge_send.at[p], edge_recv.at[slot], in_plane(p))

    def there(p, slot):
        return remote(prod_ref.at[p], recv_ref.at[slot], there_send.at[p], there_recv.at[slot], in_plane(p))

    @pl.loop(1, peers)
    def _(k):
        p = (plane + k) % peers
        there(p, plane).start()
        edges_there(p, plane).start()

    params(z, 1).start()
    rim = remote(rim_ref, rimin_ref, pair_send.at[2], pair_recv.at[2], of_all(after))
    rim.start()

    def widen(slot, value):
        for q in range(QUADS):
            at = pl.multiple_of((q * (peers + 1) + slot) * 8, 8)
            edgewide_ref[pl.ds(at, 8), :] = value[:, q * LANES : (q + 1) * LANES].astype(jnp.float32)

    def take(p, source, edges):
        spread(p, source, u_ref)
        widen(p + 1, edges[p])

    take(plane, prod_ref, edge_ref)

    @pl.loop(1, peers)
    def _(k):
        p = (plane + peers - k) % peers
        there(plane, p).wait_recv()
        edges_there(plane, p).wait_recv()
        take(p, recv_ref, edges_ref)

    params(1 - z, 0).wait_recv()
    scatter_rates(modes_ref, rate_ref)
    cross(plane).wait_recv()
    widen(0, cross_ref[...])
    repair(block * peers * rows, rows, plane, doc_ref, short_ref, edgewide_ref, u_ref)

    local_states(u_ref, rate_ref, end_ref, steps)
    block_states(end_ref, rate_ref, state_ref, steps)
    packed_ref[...] = state_ref[...].astype(jnp.bfloat16)

    def owned(b):
        return (b // 2) % owners

    def state_copy(b, slot):
        return remote(packed_ref.at[owned(b)], states_ref.at[slot], ring_send.at[b], ring_recv.at[slot], in_column(b))

    @pl.loop(1, blocks)
    def _(k):
        state_copy((block + k) % blocks, block).start()

    states_ref[block] = packed_ref[owned(block)]
    params(1 - z, 1).wait_recv()
    scatter_gains(modes_ref, gain_ref, skip_ref)
    for m in range(MODES):
        put_rows(fade_ref, m, jnp.exp(-2.0 * steps * rate_ref[m * 8 : m * 8 + 4, :]))
    zero = (jnp.zeros((8, LANES), jnp.float32),) * MODES
    local_outputs(zero, 0, steps, u_ref, rate_ref, gain_ref, skip_ref, y_ref, steps)
    rim.wait_recv()

    @pl.loop(0, 2 * peers)
    def _(i):
        form_gate(i, one, two, feat_ref, rimin_ref, short_ref, gate_ref)

    @pl.loop(1, blocks)
    def _(k):
        state_copy(block, (block + k) % blocks).wait_recv()

    fade = fade_ref[owned(block)]

    def chain(b, carry):
        carries_ref[b] = carry
        return fade * carry + states_ref[b].astype(jnp.float32)

    lax.fori_loop(0, blocks, chain, jnp.zeros_like(fade))
    group = seq // owners * owners

    def near(j):
        return group + (owned(block) + j) % owners

    def carry_copy(to, slot):
        return remote(
            carries_ref.at[to * 2 + z], carry_ref.at[slot], near_send.at[to % owners], near_recv.at[slot],
            (to, chan),
        )

    @pl.loop(1, owners)
    def _(j):
        carry_copy(near(j), owned(block)).start()

    carry_ref[owned(block)] = carries_ref[block]

    @pl.loop(1, owners)
    def _(j):
        carry_copy(seq, near(j) % owners).wait_recv()

    carried(end_ref, carry_ref, rate_ref, gain_ref, base_ref, steps)

    def back(p, slot):
        return remote(mixed_ref.at[p], back_ref.at[slot], back_send.at[p], back_recv.at[slot], in_plane(p))

    @pl.loop(0, peers // 2)
    def _(k):
        i = (plane + k) % (peers // 2)
        add_carried(i, rows, base_ref, rate_ref, y_ref, steps)
        for h in range(2):
            p = h * (peers // 2) + i
            gathered(y_ref, mixed_ref, p, h, i * rows, rows, steps)

            @pl.when(p != plane)
            def _():
                back(p, plane).start()

    def finish(p, source):
        for half in range(2):
            cols = pl.ds(pl.multiple_of((half * peers + p) * HALF, HALF), HALF)
            value = source[p, :, half * HALF : (half + 1) * HALF].astype(jnp.float32)
            out_ref[:, cols] = (gate_ref[:, cols].astype(jnp.float32) * value).astype(jnp.bfloat16)

    finish(plane, mixed_ref)

    @pl.loop(1, peers)
    def _(k):
        p = (plane + k) % peers
        back(plane, p).wait_recv()
        finish(p, back_ref)

    rim.wait_send()
    params(z, 0).wait_send()
    params(z, 1).wait_send()

    @pl.when(plane == peers - 1)
    def _():
        @pl.loop(0, peers)
        def _(p):
            cross(p).wait_send()

    @pl.loop(1, peers)
    def _(k):
        p = (plane + k) % peers
        there(p, plane).wait_send()
        edges_there(p, plane).wait_send()
        back(p, plane).wait_send()

    @pl.loop(1, blocks)
    def _(k):
        state_copy((block + k) % blocks, block).wait_send()

    @pl.loop(1, owners)
    def _(j):
        carry_copy(near(j), owned(block)).wait_send()


def per_device(features, short_weights, doc_lengths, residues, rates, skip):
    seqs = lax.axis_size("seq")
    blocks = 2 * seqs
    owners = min(8, seqs)
    peers = lax.axis_size("chan") // 2
    rows, width = features.shape[1:]
    bf16, f32 = jnp.bfloat16, jnp.float32
    vmem = pltpu.VMEM
    operands = (doc_lengths[None, :], features, short_weights, residues, rates, skip[None, :])
    wide = vmem((peers * rows * QUADS, LANES), f32)
    table = vmem((8 * MODES, LANES), f32)
    rim = vmem((2, width), bf16)
    moved = vmem((peers, rows, 2 * HALF), bf16)
    edges = vmem((peers, 8, 2 * HALF), bf16)
    height = MODES * QUADS // owners
    owned = vmem((owners, height, LANES), f32)
    dma = lambda *n: pltpu.SemaphoreType.DMA(n)
    return pl.pallas_call(
        kernel,
        out_shape=jax.ShapeDtypeStruct((rows, width), bf16),
        in_specs=[pl.BlockSpec(memory_space=pl.ANY)] * 6,
        out_specs=VMEM,
        scratch_shapes=[vmem(x.shape, x.dtype) for x in operands]
        + [
            rim, rim,
            vmem((2, 2 * MODES + 8, HALF), f32),
            vmem((rows, width), bf16),
            moved, moved, edges, edges, vmem((8, 2 * HALF), bf16), vmem((8 * QUADS * (peers + 1), LANES), f32),
            wide, wide, moved, moved,
            table, table, vmem((8, LANES), f32), table, table,
            owned, vmem((owners, height, LANES), bf16), vmem((blocks, height, LANES), bf16),
            vmem((blocks, height, LANES), f32), owned, owned,
            dma(6), dma(3), dma(4), dma(peers), dma(peers), dma(peers), dma(peers), dma(peers), dma(peers), dma(peers),
            dma(blocks), dma(blocks), dma(owners), dma(owners),
        ],
        compiler_params=pltpu.CompilerParams(
            collective_id=0, has_side_effects=True, vmem_limit_bytes=58 * 2**20
        ),
    )(*operands)


def solution(mesh):
    placed = (P(None, ("seq", "chan"), None), P(), P(), P(None, "chan"), P(None, "chan"), P("chan"))
    return jax.shard_map(
        per_device, mesh=mesh, in_specs=placed, out_specs=P(("seq", "chan"), None), check_vma=False
    )
```

```python
import jax
import jax.numpy as jnp
from jax import lax
from jax.experimental import pallas as pl
from jax.experimental.pallas import tpu as pltpu
from jax.sharding import PartitionSpec as P

MODES = 16
LANES = 128
QUADS = 4
HALF = 256
VMEM = pl.BlockSpec(memory_space=pltpu.VMEM)
MESH = pl.DeviceIdType.MESH


def doc_starts(doc_ref):
    n = doc_ref.shape[1]
    lengths = doc_ref[...].astype(jnp.float32)
    rows = lax.broadcasted_iota(jnp.int32, (n, n), 0)
    cols = lax.broadcasted_iota(jnp.int32, (n, n), 1)
    wide = jnp.broadcast_to(lengths, (n, n))
    column = jnp.sum(jnp.where(rows == cols, wide, 0.0), axis=1, keepdims=True)
    return jnp.sum(jnp.where(rows < cols, column, 0.0), axis=0, keepdims=True)


def tap_masks(first, doc_ref, rows):
    starts = doc_starts(doc_ref)
    n = starts.shape[1]
    index = lax.broadcasted_iota(jnp.int32, (rows, n), 0)
    position = (first + index).astype(jnp.float32)
    here = jnp.max(jnp.where(starts == position, 1.0, 0.0), axis=1, keepdims=True)
    before = jnp.max(jnp.where(starts == position - 1.0, 1.0, 0.0), axis=1, keepdims=True)
    one = jnp.broadcast_to(here, (rows, HALF)) < 0.5
    two = jnp.broadcast_to(here + before, (rows, HALF)) < 0.5
    return one, two


def filtered(x, x1, x2, one, two, short_ref, s, cols):
    return (
        x * short_ref[s, 0:1, cols]
        + jnp.where(one, x1, 0.0) * short_ref[s, 1:2, cols]
        + jnp.where(two, x2, 0.0) * short_ref[s, 2:3, cols]
    )


def form_product(block, one, two, feat_ref, short_ref):
    rows = one.shape[0]
    cols = pl.ds(pl.multiple_of(block * HALF, HALF), HALF)
    streams, ends = [], []
    for s in (1, 2):
        x = feat_ref[s, :, cols].astype(jnp.float32)
        ends.append((x[0:8], x[rows - 8 : rows]))
        streams.append(
            filtered(x, pltpu.roll(x, 1, 0), pltpu.roll(x, 2, 0), one, two, short_ref, s, cols)
        )
    row = lax.broadcasted_iota(jnp.int32, (8, HALF), 0)
    (key_top, key_end), (value_top, value_end) = ends
    lower = jnp.where(row < 6, pltpu.roll(value_end, 6, 0), key_end)
    upper = jnp.where(row < 2, key_top, pltpu.roll(value_top, 2, 0))
    edges = jnp.where(row < 4, upper, lower)
    return (streams[0] * streams[1]).astype(jnp.bfloat16), edges.astype(jnp.bfloat16)


def form_gate(block, one, two, feat_ref, rim_ref, short_ref, gate_ref):
    row = lax.broadcasted_iota(jnp.int32, one.shape, 0)
    cols = pl.ds(pl.multiple_of(block * HALF, HALF), HALF)
    x = feat_ref[0, :, cols].astype(jnp.float32)
    rim = rim_ref[:, cols].astype(jnp.float32)
    x1 = jnp.where(row == 0, rim[1:2], pltpu.roll(x, 1, 0))
    x2 = jnp.where(row == 0, rim[0:1], jnp.where(row == 1, rim[1:2], pltpu.roll(x, 2, 0)))
    gate_ref[:, cols] = filtered(x, x1, x2, one, two, short_ref, 0, cols).astype(jnp.bfloat16)


def repair(first, rows, plane, doc_ref, short_ref, edge_ref, u_ref):
    peers = edge_ref.shape[0] // (8 * QUADS) - 1
    steps = peers * rows // 2
    starts = doc_starts(doc_ref)
    n = starts.shape[1]
    index = lax.broadcasted_iota(jnp.int32, (peers, n), 0)
    position = (first + index * rows).astype(jnp.float32)

    def begins(shift):
        hit = jnp.where(starts == position + shift, 1.0, 0.0)
        return jnp.broadcast_to(jnp.max(hit, axis=1, keepdims=True), (peers, HALF))

    before, here, later = begins(-1.0), begins(0.0), begins(1.0)
    one = (here < 0.5, later < 0.5)
    two = (here + before < 0.5, later + here < 0.5)
    for half in range(2):
        cols = pl.ds(pl.multiple_of((half * peers + plane) * HALF, HALF), HALF)
        lanes = slice(half * HALF, (half + 1) * HALF)

        def edge(slot, r):
            parts = [
                edge_ref[pl.ds((half * 2 + i) * 8 * (peers + 1) + slot * 8 + r, peers, stride=8), :]
                for i in range(HALF // LANES)
            ]
            return jnp.concatenate(parts, axis=1)

        fixed = []
        for s, top, last in ((1, 0, 6), (2, 2, 4)):
            x = [edge(0, last), edge(0, last + 1), edge(1, top), edge(1, top + 1)]
            fixed.append(
                [
                    filtered(x[2 + i], x[1 + i], x[i], one[i], two[i], short_ref, s, cols)
                    for i in range(2)
                ]
            )
        for i in range(2):
            value = (fixed[0][i] * fixed[1][i]).astype(jnp.bfloat16).astype(jnp.float32)
            for h in range(2):
                for j in range(HALF // LANES):
                    q = half * (HALF // LANES) + j
                    at = pl.ds((h * QUADS + q) * steps + i, peers // 2, stride=rows)
                    u_ref[at, :] = value[h * (peers // 2) : (h + 1) * (peers // 2), j * LANES : (j + 1) * LANES]


def mode_gain(rate, residue):
    x = 2.0 * rate
    series = jnp.ones_like(x)
    for n in range(9, 1, -1):
        series = 1.0 - x * (1.0 / n) * series
    return residue * jnp.sqrt(x * series)


def scatter_rates(modes_ref, rate_ref):
    for q in range(QUADS):
        cols = slice((q % 2) * LANES, (q % 2 + 1) * LANES)
        for h in range(2):
            rate_ref[pl.ds(h * QUADS + q, MODES, stride=8), :] = modes_ref[q // 2, 0:MODES, cols]


def scatter_gains(modes_ref, gain_ref, skip_ref):
    for q in range(QUADS):
        cols = slice((q % 2) * LANES, (q % 2 + 1) * LANES)
        for h in range(2):
            at = h * QUADS + q
            gain_ref[pl.ds(at, MODES, stride=8), :] = modes_ref[q // 2, MODES : 2 * MODES, cols]
            skip_ref[at : at + 1, :] = modes_ref[q // 2, 2 * MODES : 2 * MODES + 1, cols]


def spread(p, recv_ref, u_ref):
    peers, rows, _ = recv_ref.shape
    steps = peers * rows // 2
    h = p // (peers // 2)
    t = (p % (peers // 2)) * rows
    for q in range(QUADS):
        at = pl.multiple_of((h * QUADS + q) * steps + t, 32)
        u_ref[pl.ds(at, rows), :] = recv_ref[p, :, q * LANES : (q + 1) * LANES].astype(jnp.float32)


def mode_rows(ref):
    return [ref[m * 8 : m * 8 + 8, :] for m in range(MODES)]


def local_states(u_ref, rate_ref, end_ref, steps):
    decay = [jnp.exp(-x) for x in mode_rows(rate_ref)]

    def step(t, x):
        u = u_ref[pl.ds(t, 8, stride=steps), :]
        return tuple(d * a + u for d, a in zip(decay, x))

    zero = jnp.zeros((8, LANES), jnp.float32)
    x = lax.fori_loop(0, steps, step, (zero,) * MODES, unroll=8)
    for m in range(MODES):
        end_ref[m * 8 : m * 8 + 8, :] = x[m]


def block_states(end_ref, rate_ref, state_ref, steps):
    for m in range(MODES):
        x = end_ref[m * 8 : m * 8 + 8, :]
        rate = rate_ref[m * 8 : m * 8 + 4, :]
        state = jnp.exp(-float(steps) * rate) * x[0:4] + x[4:8]
        put_rows(state_ref, m, state)


def put_rows(ref, m, value):
    height = ref.shape[1]
    if height <= QUADS:
        for i in range(QUADS // height):
            ref[m * (QUADS // height) + i] = value[i * height : (i + 1) * height]
    else:
        each = height // QUADS
        ref[m // each, (m % each) * QUADS : (m % each + 1) * QUADS, :] = value


def get_rows(ref, m):
    height = ref.shape[1]
    if height <= QUADS:
        n = QUADS // height
        return jnp.concatenate([ref[m * n + i] for i in range(n)], axis=0)
    each = height // QUADS
    return ref[m // each, (m % each) * QUADS : (m % each + 1) * QUADS, :]


def local_outputs(x, begin, end, u_ref, rate_ref, gain_ref, skip_ref, y_ref, steps):
    decay = [jnp.exp(-x) for x in mode_rows(rate_ref)]
    gain = mode_rows(gain_ref)
    skip = skip_ref[...]

    def step(t, x):
        u = u_ref[pl.ds(t, 8, stride=steps), :]
        x = tuple(d * a + u for d, a in zip(decay, x))
        y_ref[pl.ds(t, 8, stride=steps), :] = total([g * a for g, a in zip(gain, x)] + [skip * u])
        return x

    return lax.fori_loop(begin, end, step, x, unroll=4)


def total(parts):
    while len(parts) > 1:
        parts = [sum(parts[i : i + 2]) for i in range(0, len(parts), 2)]
    return parts[0]


def carried(end_ref, carry_ref, rate_ref, gain_ref, base_ref, steps):
    for m in range(MODES):
        carry = get_rows(carry_ref, m)
        rate = rate_ref[m * 8 : m * 8 + 4, :]
        later = end_ref[m * 8 : m * 8 + 4, :] + jnp.exp(-float(steps) * rate) * carry
        both = jnp.concatenate([carry, later], axis=0)
        base_ref[m * 8 : m * 8 + 8, :] = gain_ref[m * 8 : m * 8 + 8, :] * both


def add_carried(i, rows, base_ref, rate_ref, y_ref, steps):
    rate = mode_rows(rate_ref)
    decay = [jnp.exp(-x) for x in rate]
    begin = i * rows
    past = begin.astype(jnp.float32)
    state = tuple(a * jnp.exp(-past * r) for a, r in zip(mode_rows(base_ref), rate))

    def step(t, state):
        state = tuple(d * a for d, a in zip(decay, state))
        at = pl.ds(begin + t, 8, stride=steps)
        y_ref[at, :] = y_ref[at, :] + total(list(state))
        return state

    lax.fori_loop(0, rows, step, state, unroll=8)


def gathered(y_ref, out_ref, p, h, t, rows, steps):
    for q in range(QUADS):
        at = pl.multiple_of((h * QUADS + q) * steps + t, 32)
        out_ref[p, :, q * LANES : (q + 1) * LANES] = y_ref[pl.ds(at, rows), :].astype(jnp.bfloat16)


def kernel(
    doc_hbm, feat_hbm, short_hbm, residues_hbm, rates_hbm, skip_hbm,
    out_ref,
    doc_ref, feat_ref, short_ref, residues_ref, rates_ref, skipin_ref,
    rim_ref, rimin_ref, modes_ref, gate_ref, prod_ref, recv_ref, edge_ref, edges_ref, cross_ref, edgewide_ref,
    u_ref, y_ref, mixed_ref, back_ref,
    rate_ref, gain_ref, skip_ref, end_ref, base_ref, state_ref, packed_ref, states_ref, carries_ref, carry_ref, fade_ref,
    load, pair_send, pair_recv, cross_send, there_send, there_recv, edge_send, edge_recv, back_send, back_recv,
    ring_send, ring_recv, near_send, near_recv,
):
    seqs, chans = lax.axis_size("seq"), lax.axis_size("chan")
    seq, chan = lax.axis_index("seq"), lax.axis_index("chan")
    peers, rows, _ = prod_ref.shape
    blocks = 2 * seqs
    owners = state_ref.shape[0]
    steps = peers * rows // 2
    z, plane = chan // peers, chan % peers
    block = seq * 2 + z
    me = seq * chans + chan
    count = seqs * chans
    after, prior = (me + 1) % count, (me + count - 1) % count

    def in_plane(p):
        return (seq, z * peers + p)

    def in_column(b):
        return (b // 2, (b % 2) * peers + plane)

    def of_all(i):
        return (i // chans, i % chans)

    def remote(src, dst, send, recv, device):
        return pltpu.make_async_remote_copy(src, dst, send, recv, device_id=device, device_id_type=MESH)

    barrier = pltpu.get_barrier_semaphore()

    def greet(device):
        pl.semaphore_signal(barrier, inc=1, device_id=device, device_id_type=MESH)

    @pl.loop(1, blocks)
    def _(k):
        greet(in_column((block + k) % blocks))

    greet(of_all(prior))

    @pl.loop(1, peers)
    def _(k):
        greet(in_plane((plane + k) % peers))

    pairs = (
        (feat_hbm, feat_ref), (short_hbm, short_ref), (doc_hbm, doc_ref), (rates_hbm, rates_ref),
        (residues_hbm, residues_ref), (skip_hbm, skipin_ref),
    )
    loads = [pltpu.make_async_copy(src, dst, load.at[i]) for i, (src, dst) in enumerate(pairs)]
    for copy in loads:
        copy.start()
    for copy in loads[2:]:
        copy.wait()
    rates = rates_ref[...]
    modes_ref[z, 0:MODES, :] = rates
    modes_ref[z, MODES : 2 * MODES, :] = mode_gain(rates, residues_ref[...])
    modes_ref[z, 2 * MODES : 2 * MODES + 8, :] = jnp.broadcast_to(skipin_ref[...], (8, HALF))
    one, two = tap_masks(me * rows, doc_ref, rows)
    for copy in loads[:2]:
        copy.wait()
    rim_ref[...] = feat_ref[0, rows - 2 : rows, :]

    @pl.loop(0, peers)
    def _(p):
        for half in range(2):
            value, edges = form_product(half * peers + p, one, two, feat_ref, short_ref)
            prod_ref[p, :, half * HALF : (half + 1) * HALF] = value
            edge_ref[p, :, half * HALF : (half + 1) * HALF] = edges

    pl.semaphore_wait(barrier, peers + blocks - 1)

    partner = (seq, (1 - z) * peers + plane)

    def params(slot, part):
        at = modes_ref.at[slot, pl.ds(0, MODES)] if part == 0 else modes_ref.at[slot, pl.ds(MODES, MODES + 8)]
        return remote(at, at, pair_send.at[part], pair_recv.at[part], partner)

    params(z, 0).start()
    rim = remote(rim_ref, rimin_ref, pair_send.at[2], pair_recv.at[2], of_all(after))
    rim.start()

    def edges_there(p, slot):
        return remote(edge_ref.at[p], edges_ref.at[slot], edge_send.at[p], edge_recv.at[slot], in_plane(p))

    def there(p, slot):
        return remote(prod_ref.at[p], recv_ref.at[slot], there_send.at[p], there_recv.at[slot], in_plane(p))

    @pl.loop(1, peers)
    def _(k):
        p = (plane + k) % peers
        edges_there(p, plane).start()

    @pl.loop(1, peers)
    def _(k):
        there((plane + k) % peers, plane).start()

    params(z, 1).start()

    def widen(slot, value):
        for q in range(QUADS):
            at = pl.multiple_of((q * (peers + 1) + slot) * 8, 8)
            edgewide_ref[pl.ds(at, 8), :] = value[:, q * LANES : (q + 1) * LANES].astype(jnp.float32)

    def take(p, source):
        spread(p, source, u_ref)

    edges_ref[plane] = edge_ref[plane]
    take(plane, prod_ref)

    @pl.loop(1, peers)
    def _(k):
        p = (plane + peers - k) % peers
        edges_there(plane, p).wait_recv()

    ahead = (block + 1) % blocks

    def cross():
        return remote(edges_ref.at[peers - 1], cross_ref, cross_send, pair_recv.at[3], in_column(ahead))

    cross().start()

    @pl.loop(0, peers)
    def _(p):
        widen(p + 1, edges_ref[p])

    @pl.loop(1, peers)
    def _(k):
        p = (plane + peers - k) % peers
        there(plane, p).wait_recv()
        take(p, recv_ref)

    params(1 - z, 0).wait_recv()
    scatter_rates(modes_ref, rate_ref)
    cross().wait_recv()
    widen(0, cross_ref[...])
    repair(block * peers * rows, rows, plane, doc_ref, short_ref, edgewide_ref, u_ref)

    local_states(u_ref, rate_ref, end_ref, steps)
    block_states(end_ref, rate_ref, state_ref, steps)
    packed_ref[...] = state_ref[...].astype(jnp.bfloat16)

    def owned(b):
        return (b // 2) % owners

    def state_copy(b, slot):
        return remote(packed_ref.at[owned(b)], states_ref.at[slot], ring_send.at[b], ring_recv.at[slot], in_column(b))

    @pl.loop(1, blocks)
    def _(k):
        state_copy((block + k) % blocks, block).start()

    states_ref[block] = packed_ref[owned(block)]
    params(1 - z, 1).wait_recv()
    scatter_gains(modes_ref, gain_ref, skip_ref)
    for m in range(MODES):
        put_rows(fade_ref, m, jnp.exp(-2.0 * steps * rate_ref[m * 8 : m * 8 + 4, :]))
    zero = (jnp.zeros((8, LANES), jnp.float32),) * MODES
    local_outputs(zero, 0, steps, u_ref, rate_ref, gain_ref, skip_ref, y_ref, steps)
    rim.wait_recv()

    @pl.loop(0, 2 * peers)
    def _(i):
        form_gate(i, one, two, feat_ref, rimin_ref, short_ref, gate_ref)

    @pl.loop(1, blocks)
    def _(k):
        state_copy(block, (block + k) % blocks).wait_recv()

    fade = fade_ref[owned(block)]

    def chain(b, carry):
        carries_ref[b] = carry
        return fade * carry + states_ref[b].astype(jnp.float32)

    lax.fori_loop(0, blocks, chain, jnp.zeros_like(fade))
    group = seq // owners * owners

    def near(j):
        return group + (owned(block) + j) % owners

    def carry_copy(to, slot):
        return remote(
            carries_ref.at[to * 2 + z], carry_ref.at[slot], near_send.at[to % owners], near_recv.at[slot],
            (to, chan),
        )

    @pl.loop(1, owners)
    def _(j):
        carry_copy(near(j), owned(block)).start()

    carry_ref[owned(block)] = carries_ref[block]

    @pl.loop(1, owners)
    def _(j):
        carry_copy(seq, near(j) % owners).wait_recv()

    carried(end_ref, carry_ref, rate_ref, gain_ref, base_ref, steps)

    def back(p, slot):
        return remote(mixed_ref.at[p], back_ref.at[slot], back_send.at[p], back_recv.at[slot], in_plane(p))

    @pl.loop(0, peers // 2)
    def _(k):
        i = (plane + k) % (peers // 2)
        add_carried(i, rows, base_ref, rate_ref, y_ref, steps)
        for h in range(2):
            p = h * (peers // 2) + i
            gathered(y_ref, mixed_ref, p, h, i * rows, rows, steps)

            @pl.when(p != plane)
            def _():
                back(p, plane).start()

    def finish(p, source):
        for half in range(2):
            cols = pl.ds(pl.multiple_of((half * peers + p) * HALF, HALF), HALF)
            value = source[p, :, half * HALF : (half + 1) * HALF].astype(jnp.float32)
            out_ref[:, cols] = (gate_ref[:, cols].astype(jnp.float32) * value).astype(jnp.bfloat16)

    finish(plane, mixed_ref)

    @pl.loop(1, peers)
    def _(k):
        p = (plane + k) % peers
        back(plane, p).wait_recv()
        finish(p, back_ref)

    rim.wait_send()
    params(z, 0).wait_send()
    params(z, 1).wait_send()

    cross().wait_send()

    @pl.loop(1, peers)
    def _(k):
        p = (plane + k) % peers
        there(p, plane).wait_send()
        edges_there(p, plane).wait_send()
        back(p, plane).wait_send()

    @pl.loop(1, blocks)
    def _(k):
        state_copy((block + k) % blocks, block).wait_send()

    @pl.loop(1, owners)
    def _(j):
        carry_copy(near(j), owned(block)).wait_send()


def per_device(features, short_weights, doc_lengths, residues, rates, skip):
    seqs = lax.axis_size("seq")
    blocks = 2 * seqs
    owners = min(8, seqs)
    peers = lax.axis_size("chan") // 2
    rows, width = features.shape[1:]
    bf16, f32 = jnp.bfloat16, jnp.float32
    vmem = pltpu.VMEM
    operands = (doc_lengths[None, :], features, short_weights, residues, rates, skip[None, :])
    wide = vmem((peers * rows * QUADS, LANES), f32)
    table = vmem((8 * MODES, LANES), f32)
    rim = vmem((2, width), bf16)
    moved = vmem((peers, rows, 2 * HALF), bf16)
    edges = vmem((peers, 8, 2 * HALF), bf16)
    height = MODES * QUADS // owners
    owned = vmem((owners, height, LANES), f32)
    dma = lambda *n: pltpu.SemaphoreType.DMA(n)
    return pl.pallas_call(
        kernel,
        out_shape=jax.ShapeDtypeStruct((rows, width), bf16),
        in_specs=[pl.BlockSpec(memory_space=pl.ANY)] * 6,
        out_specs=VMEM,
        scratch_shapes=[vmem(x.shape, x.dtype) for x in operands]
        + [
            rim, rim,
            vmem((2, 2 * MODES + 8, HALF), f32),
            vmem((rows, width), bf16),
            moved, moved, edges, edges, vmem((8, 2 * HALF), bf16), vmem((8 * QUADS * (peers + 1), LANES), f32),
            wide, wide, moved, moved,
            table, table, vmem((8, LANES), f32), table, table,
            owned, vmem((owners, height, LANES), bf16), vmem((blocks, height, LANES), bf16),
            vmem((blocks, height, LANES), f32), owned, owned,
            dma(6), dma(3), dma(4), pltpu.SemaphoreType.DMA, dma(peers), dma(peers), dma(peers), dma(peers), dma(peers), dma(peers),
            dma(blocks), dma(blocks), dma(owners), dma(owners),
        ],
        compiler_params=pltpu.CompilerParams(
            collective_id=0, has_side_effects=True, vmem_limit_bytes=58 * 2**20
        ),
    )(*operands)


def solution(mesh):
    placed = (P(None, ("seq", "chan"), None), P(), P(), P(None, "chan"), P(None, "chan"), P("chan"))
    return jax.shard_map(
        per_device, mesh=mesh, in_specs=placed, out_specs=P(("seq", "chan"), None), check_vma=False
    )
```

```python
import jax
import jax.numpy as jnp
from jax import lax
from jax.experimental import pallas as pl
from jax.experimental.pallas import tpu as pltpu
from jax.sharding import PartitionSpec as P

MODES = 16
LANES = 128
QUADS = 4
HALF = 256
VMEM = pl.BlockSpec(memory_space=pltpu.VMEM)
MESH = pl.DeviceIdType.MESH


def doc_starts(doc_ref):
    n = doc_ref.shape[1]
    lengths = doc_ref[...].astype(jnp.float32)
    rows = lax.broadcasted_iota(jnp.int32, (n, n), 0)
    cols = lax.broadcasted_iota(jnp.int32, (n, n), 1)
    wide = jnp.broadcast_to(lengths, (n, n))
    column = jnp.sum(jnp.where(rows == cols, wide, 0.0), axis=1, keepdims=True)
    return jnp.sum(jnp.where(rows < cols, column, 0.0), axis=0, keepdims=True)


def tap_masks(first, doc_ref, rows):
    starts = doc_starts(doc_ref)
    n = starts.shape[1]
    index = lax.broadcasted_iota(jnp.int32, (rows, n), 0)
    position = (first + index).astype(jnp.float32)
    here = jnp.max(jnp.where(starts == position, 1.0, 0.0), axis=1, keepdims=True)
    before = jnp.max(jnp.where(starts == position - 1.0, 1.0, 0.0), axis=1, keepdims=True)
    one = jnp.broadcast_to(here, (rows, HALF)) < 0.5
    two = jnp.broadcast_to(here + before, (rows, HALF)) < 0.5
    return one, two


def filtered(x, x1, x2, one, two, short_ref, s, cols):
    return (
        x * short_ref[s, 0:1, cols]
        + jnp.where(one, x1, 0.0) * short_ref[s, 1:2, cols]
        + jnp.where(two, x2, 0.0) * short_ref[s, 2:3, cols]
    )


def form_product(block, one, two, feat_ref, short_ref):
    cols = pl.ds(pl.multiple_of(block * HALF, HALF), HALF)
    streams = []
    for s in (1, 2):
        x = feat_ref[s, :, cols].astype(jnp.float32)
        streams.append(
            filtered(x, pltpu.roll(x, 1, 0), pltpu.roll(x, 2, 0), one, two, short_ref, s, cols)
        )
    return (streams[0] * streams[1]).astype(jnp.bfloat16)


def form_edges(block, feat_ref):
    rows = feat_ref.shape[1]
    cols = pl.ds(pl.multiple_of(block * HALF, HALF), HALF)
    row = lax.broadcasted_iota(jnp.int32, (8, HALF), 0)
    (key_top, key_end), (value_top, value_end) = [
        (
            feat_ref[s, 0:16, cols].astype(jnp.float32)[0:8],
            feat_ref[s, rows - 16 : rows, cols].astype(jnp.float32)[8:16],
        )
        for s in (1, 2)
    ]
    lower = jnp.where(row < 6, pltpu.roll(value_end, 6, 0), key_end)
    upper = jnp.where(row < 2, key_top, pltpu.roll(value_top, 2, 0))
    return jnp.where(row < 4, upper, lower).astype(jnp.bfloat16)


def form_gate(block, one, two, feat_ref, short_ref, gate_ref):
    cols = pl.ds(pl.multiple_of(block * HALF, HALF), HALF)
    x = feat_ref[0, :, cols].astype(jnp.float32)
    gate = filtered(x, pltpu.roll(x, 1, 0), pltpu.roll(x, 2, 0), one, two, short_ref, 0, cols)
    gate_ref[:, cols] = gate.astype(jnp.bfloat16)


def repair_gate(block, one, two, feat_ref, rim_ref, short_ref, gate_ref):
    row = lax.broadcasted_iota(jnp.int32, (16, HALF), 0)
    cols = pl.ds(pl.multiple_of(block * HALF, HALF), HALF)
    x = feat_ref[0, 0:16, cols].astype(jnp.float32)
    rim = rim_ref[:, cols].astype(jnp.float32)
    x1 = jnp.where(row == 0, rim[1:2], pltpu.roll(x, 1, 0))
    x2 = jnp.where(row == 0, rim[0:1], jnp.where(row == 1, rim[1:2], pltpu.roll(x, 2, 0)))
    gate = filtered(x, x1, x2, one[0:16], two[0:16], short_ref, 0, cols)
    gate_ref[0:16, cols] = gate.astype(jnp.bfloat16)


def repair(first, rows, plane, doc_ref, short_ref, edge_ref, u_ref):
    peers = edge_ref.shape[0] // (8 * QUADS) - 1
    steps = peers * rows // 2
    starts = doc_starts(doc_ref)
    n = starts.shape[1]
    index = lax.broadcasted_iota(jnp.int32, (peers, n), 0)
    position = (first + index * rows).astype(jnp.float32)

    def begins(shift):
        hit = jnp.where(starts == position + shift, 1.0, 0.0)
        return jnp.broadcast_to(jnp.max(hit, axis=1, keepdims=True), (peers, HALF))

    before, here, later = begins(-1.0), begins(0.0), begins(1.0)
    one = (here < 0.5, later < 0.5)
    two = (here + before < 0.5, later + here < 0.5)
    for half in range(2):
        cols = pl.ds(pl.multiple_of((half * peers + plane) * HALF, HALF), HALF)
        lanes = slice(half * HALF, (half + 1) * HALF)

        def edge(slot, r):
            parts = [
                edge_ref[pl.ds((half * 2 + i) * 8 * (peers + 1) + slot * 8 + r, peers, stride=8), :]
                for i in range(HALF // LANES)
            ]
            return jnp.concatenate(parts, axis=1)

        fixed = []
        for s, top, last in ((1, 0, 6), (2, 2, 4)):
            x = [edge(0, last), edge(0, last + 1), edge(1, top), edge(1, top + 1)]
            fixed.append(
                [
                    filtered(x[2 + i], x[1 + i], x[i], one[i], two[i], short_ref, s, cols)
                    for i in range(2)
                ]
            )
        for i in range(2):
            value = (fixed[0][i] * fixed[1][i]).astype(jnp.bfloat16).astype(jnp.float32)
            for h in range(2):
                for j in range(HALF // LANES):
                    q = half * (HALF // LANES) + j
                    at = pl.ds((h * QUADS + q) * steps + i, peers // 2, stride=rows)
                    u_ref[at, :] = value[h * (peers // 2) : (h + 1) * (peers // 2), j * LANES : (j + 1) * LANES]


def mode_gain(rate, residue):
    x = 2.0 * rate
    series = jnp.ones_like(x)
    for n in range(9, 1, -1):
        series = 1.0 - x * (1.0 / n) * series
    return residue * jnp.sqrt(x * series)


def scatter_rates(modes_ref, rate_ref):
    for q in range(QUADS):
        cols = slice((q % 2) * LANES, (q % 2 + 1) * LANES)
        for h in range(2):
            rate_ref[pl.ds(h * QUADS + q, MODES, stride=8), :] = modes_ref[q // 2, 0:MODES, cols]


def scatter_gains(modes_ref, gain_ref, skip_ref):
    for q in range(QUADS):
        cols = slice((q % 2) * LANES, (q % 2 + 1) * LANES)
        for h in range(2):
            at = h * QUADS + q
            gain_ref[pl.ds(at, MODES, stride=8), :] = modes_ref[q // 2, MODES : 2 * MODES, cols]
            skip_ref[at : at + 1, :] = modes_ref[q // 2, 2 * MODES : 2 * MODES + 1, cols]


def spread(p, recv_ref, u_ref):
    peers, rows, _ = recv_ref.shape
    steps = peers * rows // 2
    h = p // (peers // 2)
    t = (p % (peers // 2)) * rows
    for q in range(QUADS):
        at = pl.multiple_of((h * QUADS + q) * steps + t, 32)
        u_ref[pl.ds(at, rows), :] = recv_ref[p, :, q * LANES : (q + 1) * LANES].astype(jnp.float32)


def mode_rows(ref):
    return [ref[m * 8 : m * 8 + 8, :] for m in range(MODES)]


def local_states(u_ref, rate_ref, end_ref, steps):
    decay = [jnp.exp(-x) for x in mode_rows(rate_ref)]

    def step(t, x):
        u = u_ref[pl.ds(t, 8, stride=steps), :]
        return tuple(d * a + u for d, a in zip(decay, x))

    zero = jnp.zeros((8, LANES), jnp.float32)
    x = lax.fori_loop(0, steps, step, (zero,) * MODES, unroll=8)
    for m in range(MODES):
        end_ref[m * 8 : m * 8 + 8, :] = x[m]


def block_states(end_ref, rate_ref, state_ref, steps):
    for m in range(MODES):
        x = end_ref[m * 8 : m * 8 + 8, :]
        rate = rate_ref[m * 8 : m * 8 + 4, :]
        state = jnp.exp(-float(steps) * rate) * x[0:4] + x[4:8]
        put_rows(state_ref, m, state)


def put_rows(ref, m, value):
    height = ref.shape[1]
    if height <= QUADS:
        for i in range(QUADS // height):
            ref[m * (QUADS // height) + i] = value[i * height : (i + 1) * height]
    else:
        each = height // QUADS
        ref[m // each, (m % each) * QUADS : (m % each + 1) * QUADS, :] = value


def get_rows(ref, m):
    height = ref.shape[1]
    if height <= QUADS:
        n = QUADS // height
        return jnp.concatenate([ref[m * n + i] for i in range(n)], axis=0)
    each = height // QUADS
    return ref[m // each, (m % each) * QUADS : (m % each + 1) * QUADS, :]


def local_outputs(x, begin, end, u_ref, rate_ref, gain_ref, skip_ref, y_ref, steps):
    decay = [jnp.exp(-x) for x in mode_rows(rate_ref)]
    gain = mode_rows(gain_ref)
    skip = skip_ref[...]

    def step(t, x):
        u = u_ref[pl.ds(t, 8, stride=steps), :]
        x = tuple(d * a + u for d, a in zip(decay, x))
        y_ref[pl.ds(t, 8, stride=steps), :] = total([g * a for g, a in zip(gain, x)] + [skip * u])
        return x

    return lax.fori_loop(begin, end, step, x, unroll=4)


def total(parts):
    while len(parts) > 1:
        parts = [sum(parts[i : i + 2]) for i in range(0, len(parts), 2)]
    return parts[0]


def carried(end_ref, carry_ref, rate_ref, gain_ref, base_ref, steps):
    for m in range(MODES):
        carry = get_rows(carry_ref, m)
        rate = rate_ref[m * 8 : m * 8 + 4, :]
        later = end_ref[m * 8 : m * 8 + 4, :] + jnp.exp(-float(steps) * rate) * carry
        both = jnp.concatenate([carry, later], axis=0)
        base_ref[m * 8 : m * 8 + 8, :] = gain_ref[m * 8 : m * 8 + 8, :] * both


def add_carried(i, rows, base_ref, rate_ref, y_ref, steps):
    rate = mode_rows(rate_ref)
    decay = [jnp.exp(-x) for x in rate]
    begin = i * rows
    past = begin.astype(jnp.float32)
    state = tuple(a * jnp.exp(-past * r) for a, r in zip(mode_rows(base_ref), rate))

    def step(t, state):
        state = tuple(d * a for d, a in zip(decay, state))
        at = pl.ds(begin + t, 8, stride=steps)
        y_ref[at, :] = y_ref[at, :] + total(list(state))
        return state

    lax.fori_loop(0, rows, step, state, unroll=8)


def gathered(y_ref, out_ref, p, h, t, rows, steps):
    for q in range(QUADS):
        at = pl.multiple_of((h * QUADS + q) * steps + t, 32)
        out_ref[p, :, q * LANES : (q + 1) * LANES] = y_ref[pl.ds(at, rows), :].astype(jnp.bfloat16)


def kernel(
    doc_hbm, feat_hbm, short_hbm, residues_hbm, rates_hbm, skip_hbm,
    out_ref,
    doc_ref, feat_ref, short_ref, residues_ref, rates_ref, skipin_ref,
    rim_ref, rimin_ref, modes_ref, gate_ref, prod_ref, recv_ref, edge_ref, edges_ref, cross_ref, edgewide_ref,
    u_ref, y_ref, mixed_ref, back_ref,
    rate_ref, gain_ref, skip_ref, end_ref, base_ref, state_ref, packed_ref, states_ref, carries_ref, carry_ref, fade_ref,
    load, pair_send, pair_recv, cross_send, there_send, there_recv, edge_send, edge_recv, back_send, back_recv,
    ring_send, ring_recv, near_send, near_recv,
):
    seqs, chans = lax.axis_size("seq"), lax.axis_size("chan")
    seq, chan = lax.axis_index("seq"), lax.axis_index("chan")
    peers, rows, _ = prod_ref.shape
    blocks = 2 * seqs
    owners = state_ref.shape[0]
    steps = peers * rows // 2
    z, plane = chan // peers, chan % peers
    block = seq * 2 + z
    me = seq * chans + chan
    count = seqs * chans
    after, prior = (me + 1) % count, (me + count - 1) % count

    def in_plane(p):
        return (seq, z * peers + p)

    def in_column(b):
        return (b // 2, (b % 2) * peers + plane)

    def of_all(i):
        return (i // chans, i % chans)

    def remote(src, dst, send, recv, device):
        return pltpu.make_async_remote_copy(src, dst, send, recv, device_id=device, device_id_type=MESH)

    barrier = pltpu.get_barrier_semaphore()

    def greet(device):
        pl.semaphore_signal(barrier, inc=1, device_id=device, device_id_type=MESH)

    pairs = (
        (feat_hbm.at[pl.ds(1, 2)], feat_ref.at[pl.ds(1, 2)]), (short_hbm, short_ref),
        (doc_hbm, doc_ref), (rates_hbm, rates_ref), (residues_hbm, residues_ref), (skip_hbm, skipin_ref),
        (feat_hbm.at[0], feat_ref.at[0]),
    )
    loads = [pltpu.make_async_copy(src, dst, load.at[i]) for i, (src, dst) in enumerate(pairs)]
    for copy in loads:
        copy.start()

    @pl.loop(1, blocks)
    def _(k):
        greet(in_column((block + k) % blocks))

    greet(of_all(prior))

    @pl.loop(1, peers)
    def _(k):
        greet(in_plane((plane + k) % peers))

    for copy in loads[2:6]:
        copy.wait()
    rates = rates_ref[...]
    modes_ref[z, 0:MODES, :] = rates
    modes_ref[z, MODES : 2 * MODES, :] = mode_gain(rates, residues_ref[...])
    modes_ref[z, 2 * MODES : 2 * MODES + 8, :] = jnp.broadcast_to(skipin_ref[...], (8, HALF))
    one, two = tap_masks(me * rows, doc_ref, rows)
    for copy in loads[:2]:
        copy.wait()

    @pl.loop(0, peers)
    def _(p):
        for half in range(2):
            edge_ref[p, :, half * HALF : (half + 1) * HALF] = form_edges(half * peers + p, feat_ref)

    def make(k):
        p = (plane + k) % peers
        for half in range(2):
            value = form_product(half * peers + p, one, two, feat_ref, short_ref)
            prod_ref[p, :, half * HALF : (half + 1) * HALF] = value

    soon = peers // 2
    pl.loop(1, soon)(make)
    loads[6].wait()
    rim_ref[...] = feat_ref[0, rows - 2 : rows, :]

    pl.semaphore_wait(barrier, peers + blocks - 1)

    partner = (seq, (1 - z) * peers + plane)

    def params(slot, part):
        at = modes_ref.at[slot, pl.ds(0, MODES)] if part == 0 else modes_ref.at[slot, pl.ds(MODES, MODES + 8)]
        return remote(at, at, pair_send.at[part], pair_recv.at[part], partner)

    params(z, 0).start()

    def edges_there(p, slot):
        return remote(edge_ref.at[p], edges_ref.at[slot], edge_send.at[p], edge_recv.at[slot], in_plane(p))

    def there(p, slot):
        return remote(prod_ref.at[p], recv_ref.at[slot], there_send.at[p], there_recv.at[slot], in_plane(p))

    @pl.loop(1, peers)
    def _(k):
        p = (plane + k) % peers
        edges_there(p, plane).start()

    def send(k):
        there((plane + k) % peers, plane).start()

    early = min(6, soon)
    pl.loop(1, early)(send)
    pl.loop(soon, peers + 1)(make)
    edges_ref[plane] = edge_ref[plane]
    last = peers - 1

    @pl.when(plane != last)
    def _():
        edges_there(plane, last).wait_recv()

    def cross():
        ahead = in_column((block + 1) % blocks)
        return remote(edges_ref.at[last], cross_ref, cross_send, pair_recv.at[3], ahead)

    cross().start()
    pl.loop(early, peers)(send)
    rim = remote(rim_ref, rimin_ref, pair_send.at[2], pair_recv.at[2], of_all(after))
    rim.start()
    params(z, 1).start()

    @pl.loop(0, 2 * peers)
    def _(i):
        form_gate(i, one, two, feat_ref, short_ref, gate_ref)

    def widen(slot, value):
        for q in range(QUADS):
            at = pl.multiple_of((q * (peers + 1) + slot) * 8, 8)
            edgewide_ref[pl.ds(at, 8), :] = value[:, q * LANES : (q + 1) * LANES].astype(jnp.float32)

    spread(plane, prod_ref, u_ref)

    @pl.loop(0, peers)
    def _(p):
        @pl.when((p != last) & (p != plane))
        def _():
            edges_there(plane, p).wait_recv()

        widen(p + 1, edges_ref[p])

    @pl.loop(1, peers)
    def _(k):
        p = (plane + peers - k) % peers
        there(plane, p).wait_recv()
        spread(p, recv_ref, u_ref)

    params(1 - z, 0).wait_recv()
    scatter_rates(modes_ref, rate_ref)
    cross().wait_recv()
    widen(0, cross_ref[...])
    repair(block * peers * rows, rows, plane, doc_ref, short_ref, edgewide_ref, u_ref)

    local_states(u_ref, rate_ref, end_ref, steps)
    block_states(end_ref, rate_ref, state_ref, steps)
    packed_ref[...] = state_ref[...].astype(jnp.bfloat16)

    def owned(b):
        return (b // 2) % owners

    def state_copy(b, slot):
        return remote(packed_ref.at[owned(b)], states_ref.at[slot], ring_send.at[b], ring_recv.at[slot], in_column(b))

    @pl.loop(1, blocks)
    def _(k):
        state_copy((block + k) % blocks, block).start()

    states_ref[block] = packed_ref[owned(block)]
    params(1 - z, 1).wait_recv()
    scatter_gains(modes_ref, gain_ref, skip_ref)
    for m in range(MODES):
        put_rows(fade_ref, m, jnp.exp(-2.0 * steps * rate_ref[m * 8 : m * 8 + 4, :]))
    zero = (jnp.zeros((8, LANES), jnp.float32),) * MODES
    local_outputs(zero, 0, steps, u_ref, rate_ref, gain_ref, skip_ref, y_ref, steps)
    @pl.loop(1, blocks)
    def _(k):
        state_copy(block, (block + k) % blocks).wait_recv()

    fade = fade_ref[owned(block)]

    def chain(b, carry):
        carries_ref[b] = carry
        return fade * carry + states_ref[b].astype(jnp.float32)

    lax.fori_loop(0, blocks, chain, jnp.zeros_like(fade))
    group = seq // owners * owners

    def near(j):
        return group + (owned(block) + j) % owners

    def carry_copy(to, slot):
        return remote(
            carries_ref.at[to * 2 + z], carry_ref.at[slot], near_send.at[to % owners], near_recv.at[slot],
            (to, chan),
        )

    @pl.loop(1, owners)
    def _(j):
        carry_copy(near(j), owned(block)).start()

    carry_ref[owned(block)] = carries_ref[block]
    rim.wait_recv()

    @pl.loop(0, 2 * peers)
    def _(i):
        repair_gate(i, one, two, feat_ref, rimin_ref, short_ref, gate_ref)

    @pl.loop(1, owners)
    def _(j):
        carry_copy(seq, near(j) % owners).wait_recv()

    carried(end_ref, carry_ref, rate_ref, gain_ref, base_ref, steps)

    def back(p, slot):
        return remote(mixed_ref.at[p], back_ref.at[slot], back_send.at[p], back_recv.at[slot], in_plane(p))

    @pl.loop(0, peers // 2)
    def _(k):
        i = (plane + k) % (peers // 2)
        add_carried(i, rows, base_ref, rate_ref, y_ref, steps)
        for h in range(2):
            p = h * (peers // 2) + i
            gathered(y_ref, mixed_ref, p, h, i * rows, rows, steps)

            @pl.when(p != plane)
            def _():
                back(p, plane).start()

    def finish(p, source):
        for half in range(2):
            cols = pl.ds(pl.multiple_of((half * peers + p) * HALF, HALF), HALF)
            value = source[p, :, half * HALF : (half + 1) * HALF].astype(jnp.float32)
            out_ref[:, cols] = (gate_ref[:, cols].astype(jnp.float32) * value).astype(jnp.bfloat16)

    finish(plane, mixed_ref)

    @pl.loop(1, peers)
    def _(k):
        p = (plane + k) % peers
        back(plane, p).wait_recv()
        finish(p, back_ref)

    rim.wait_send()
    params(z, 0).wait_send()
    params(z, 1).wait_send()

    cross().wait_send()

    @pl.loop(1, peers)
    def _(k):
        p = (plane + k) % peers
        there(p, plane).wait_send()
        edges_there(p, plane).wait_send()
        back(p, plane).wait_send()

    @pl.loop(1, blocks)
    def _(k):
        state_copy((block + k) % blocks, block).wait_send()

    @pl.loop(1, owners)
    def _(j):
        carry_copy(near(j), owned(block)).wait_send()


def per_device(features, short_weights, doc_lengths, residues, rates, skip):
    seqs = lax.axis_size("seq")
    blocks = 2 * seqs
    owners = min(8, seqs)
    peers = lax.axis_size("chan") // 2
    rows, width = features.shape[1:]
    bf16, f32 = jnp.bfloat16, jnp.float32
    vmem = pltpu.VMEM
    operands = (doc_lengths[None, :], features, short_weights, residues, rates, skip[None, :])
    wide = vmem((peers * rows * QUADS, LANES), f32)
    table = vmem((8 * MODES, LANES), f32)
    rim = vmem((2, width), bf16)
    moved = vmem((peers, rows, 2 * HALF), bf16)
    edges = vmem((peers, 8, 2 * HALF), bf16)
    height = MODES * QUADS // owners
    owned = vmem((owners, height, LANES), f32)
    dma = lambda *n: pltpu.SemaphoreType.DMA(n)
    return pl.pallas_call(
        kernel,
        out_shape=pltpu.VMEM((rows, width), bf16),
        in_specs=[pl.BlockSpec(memory_space=pl.ANY)] * 6,
        out_specs=VMEM,
        scratch_shapes=[vmem(x.shape, x.dtype) for x in operands]
        + [
            rim, rim,
            vmem((2, 2 * MODES + 8, HALF), f32),
            vmem((rows, width), bf16),
            moved, moved, edges, edges, vmem((8, 2 * HALF), bf16), vmem((8 * QUADS * (peers + 1), LANES), f32),
            wide, wide, moved, moved,
            table, table, vmem((8, LANES), f32), table, table,
            owned, vmem((owners, height, LANES), bf16), vmem((blocks, height, LANES), bf16),
            vmem((blocks, height, LANES), f32), owned, owned,
            dma(7), dma(3), dma(4), pltpu.SemaphoreType.DMA, dma(peers), dma(peers), dma(peers), dma(peers), dma(peers), dma(peers),
            dma(blocks), dma(blocks), dma(owners), dma(owners),
        ],
        compiler_params=pltpu.CompilerParams(
            collective_id=0, has_side_effects=True, vmem_limit_bytes=58 * 2**20
        ),
    )(*operands)


def solution(mesh):
    placed = (P(None, ("seq", "chan"), None), P(), P(), P(None, "chan"), P(None, "chan"), P("chan"))
    return jax.shard_map(
        per_device, mesh=mesh, in_specs=placed, out_specs=P(("seq", "chan"), None), check_vma=False
    )
```

```python
import jax
import jax.numpy as jnp
from jax import lax
from jax.experimental import pallas as pl
from jax.experimental.pallas import tpu as pltpu
from jax.sharding import PartitionSpec as P

MODES = 16
EDGES = 8
LANES = 128
QUADS = 4
HALF = 256
VMEM = pl.BlockSpec(memory_space=pltpu.VMEM)
MESH = pl.DeviceIdType.MESH


def doc_starts(doc_ref):
    n = doc_ref.shape[1]
    lengths = doc_ref[...].astype(jnp.float32)
    rows = lax.broadcasted_iota(jnp.int32, (n, n), 0)
    cols = lax.broadcasted_iota(jnp.int32, (n, n), 1)
    wide = jnp.broadcast_to(lengths, (n, n))
    column = jnp.sum(jnp.where(rows == cols, wide, 0.0), axis=1, keepdims=True)
    return jnp.sum(jnp.where(rows < cols, column, 0.0), axis=0, keepdims=True)


def tap_masks(first, doc_ref, rows):
    starts = doc_starts(doc_ref)
    n = starts.shape[1]
    index = lax.broadcasted_iota(jnp.int32, (rows, n), 0)
    position = (first + index).astype(jnp.float32)
    here = jnp.max(jnp.where(starts == position, 1.0, 0.0), axis=1, keepdims=True)
    before = jnp.max(jnp.where(starts == position - 1.0, 1.0, 0.0), axis=1, keepdims=True)
    one = jnp.broadcast_to(here, (rows, HALF)) < 0.5
    two = jnp.broadcast_to(here + before, (rows, HALF)) < 0.5
    return one, two


def filtered(x, x1, x2, one, two, short_ref, s, cols):
    return (
        x * short_ref[s, 0:1, cols]
        + jnp.where(one, x1, 0.0) * short_ref[s, 1:2, cols]
        + jnp.where(two, x2, 0.0) * short_ref[s, 2:3, cols]
    )


def form_product(block, one, two, feat_ref, short_ref):
    cols = pl.ds(pl.multiple_of(block * HALF, HALF), HALF)
    streams = []
    for s in (1, 2):
        x = feat_ref[s, :, cols].astype(jnp.float32)
        streams.append(
            filtered(x, pltpu.roll(x, 1, 0), pltpu.roll(x, 2, 0), one, two, short_ref, s, cols)
        )
    return (streams[0] * streams[1]).astype(jnp.bfloat16)


def form_edges(block, feat_ref):
    rows = feat_ref.shape[1]
    cols = pl.ds(pl.multiple_of(block * HALF, HALF), HALF)
    row = lax.broadcasted_iota(jnp.int32, (8, HALF), 0)
    (key_top, key_end), (value_top, value_end) = [
        (
            feat_ref[s, 0:16, cols].astype(jnp.float32)[0:8],
            feat_ref[s, rows - 16 : rows, cols].astype(jnp.float32)[8:16],
        )
        for s in (1, 2)
    ]
    lower = jnp.where(row < 6, pltpu.roll(value_end, 6, 0), key_end)
    upper = jnp.where(row < 2, key_top, pltpu.roll(value_top, 2, 0))
    return jnp.where(row < 4, upper, lower).astype(jnp.bfloat16)


def form_gate(block, one, two, feat_ref, short_ref, gate_ref):
    cols = pl.ds(pl.multiple_of(block * HALF, HALF), HALF)
    x = feat_ref[0, :, cols].astype(jnp.float32)
    gate = filtered(x, pltpu.roll(x, 1, 0), pltpu.roll(x, 2, 0), one, two, short_ref, 0, cols)
    gate_ref[:, cols] = gate.astype(jnp.bfloat16)


def repair_gate(block, one, two, feat_ref, rim_ref, short_ref, gate_ref):
    row = lax.broadcasted_iota(jnp.int32, (16, HALF), 0)
    cols = pl.ds(pl.multiple_of(block * HALF, HALF), HALF)
    x = feat_ref[0, 0:16, cols].astype(jnp.float32)
    rim = rim_ref[:, cols].astype(jnp.float32)
    x1 = jnp.where(row == 0, rim[1:2], pltpu.roll(x, 1, 0))
    x2 = jnp.where(row == 0, rim[0:1], jnp.where(row == 1, rim[1:2], pltpu.roll(x, 2, 0)))
    gate = filtered(x, x1, x2, one[0:16], two[0:16], short_ref, 0, cols)
    gate_ref[0:16, cols] = gate.astype(jnp.bfloat16)


def repair(first, rows, plane, doc_ref, short_ref, edge_ref, u_ref):
    peers = edge_ref.shape[0] // (8 * QUADS) - 1
    steps = peers * rows // 2
    starts = doc_starts(doc_ref)
    n = starts.shape[1]
    index = lax.broadcasted_iota(jnp.int32, (peers, n), 0)
    position = (first + index * rows).astype(jnp.float32)

    def begins(shift):
        hit = jnp.where(starts == position + shift, 1.0, 0.0)
        return jnp.broadcast_to(jnp.max(hit, axis=1, keepdims=True), (peers, HALF))

    before, here, later = begins(-1.0), begins(0.0), begins(1.0)
    one = (here < 0.5, later < 0.5)
    two = (here + before < 0.5, later + here < 0.5)
    for half in range(2):
        cols = pl.ds(pl.multiple_of((half * peers + plane) * HALF, HALF), HALF)
        lanes = slice(half * HALF, (half + 1) * HALF)

        def edge(slot, r):
            parts = [
                edge_ref[pl.ds((half * 2 + i) * 8 * (peers + 1) + slot * 8 + r, peers, stride=8), :]
                for i in range(HALF // LANES)
            ]
            return jnp.concatenate(parts, axis=1)

        fixed = []
        for s, top, last in ((1, 0, 6), (2, 2, 4)):
            x = [edge(0, last), edge(0, last + 1), edge(1, top), edge(1, top + 1)]
            fixed.append(
                [
                    filtered(x[2 + i], x[1 + i], x[i], one[i], two[i], short_ref, s, cols)
                    for i in range(2)
                ]
            )
        for i in range(2):
            value = (fixed[0][i] * fixed[1][i]).astype(jnp.bfloat16).astype(jnp.float32)
            for h in range(2):
                for j in range(HALF // LANES):
                    q = half * (HALF // LANES) + j
                    at = pl.ds((h * QUADS + q) * steps + i, peers // 2, stride=rows)
                    u_ref[at, :] = value[h * (peers // 2) : (h + 1) * (peers // 2), j * LANES : (j + 1) * LANES]


def mode_gain(rate, residue):
    x = 2.0 * rate
    series = jnp.ones_like(x)
    for n in range(9, 1, -1):
        series = 1.0 - x * (1.0 / n) * series
    return residue * jnp.sqrt(x * series)


def scatter_rates(modes_ref, rate_ref):
    for q in range(QUADS):
        cols = slice((q % 2) * LANES, (q % 2 + 1) * LANES)
        for h in range(2):
            rate_ref[pl.ds(h * QUADS + q, MODES, stride=8), :] = modes_ref[q // 2, 0:MODES, cols]


def scatter_gains(modes_ref, gain_ref, skip_ref):
    for q in range(QUADS):
        cols = slice((q % 2) * LANES, (q % 2 + 1) * LANES)
        for h in range(2):
            at = h * QUADS + q
            gain_ref[pl.ds(at, MODES, stride=8), :] = modes_ref[q // 2, MODES : 2 * MODES, cols]
            skip_ref[at : at + 1, :] = modes_ref[q // 2, 2 * MODES : 2 * MODES + 1, cols]


def spread(p, recv_ref, u_ref):
    peers, height, _ = recv_ref.shape
    rows = height - EDGES
    steps = peers * rows // 2
    h = p // (peers // 2)
    t = (p % (peers // 2)) * rows
    for q in range(QUADS):
        at = pl.multiple_of((h * QUADS + q) * steps + t, 32)
        u_ref[pl.ds(at, rows), :] = recv_ref[p, 0:rows, q * LANES : (q + 1) * LANES].astype(jnp.float32)


def mode_rows(ref):
    return [ref[m * 8 : m * 8 + 8, :] for m in range(MODES)]


def local_states(u_ref, rate_ref, end_ref, steps):
    decay = [jnp.exp(-x) for x in mode_rows(rate_ref)]

    def step(t, x):
        u = u_ref[pl.ds(t, 8, stride=steps), :]
        return tuple(d * a + u for d, a in zip(decay, x))

    zero = jnp.zeros((8, LANES), jnp.float32)
    x = lax.fori_loop(0, steps, step, (zero,) * MODES, unroll=8)
    for m in range(MODES):
        end_ref[m * 8 : m * 8 + 8, :] = x[m]


def add_first(u_ref, rate_ref, end_ref, steps):
    half = lax.broadcasted_iota(jnp.int32, (8, LANES), 0) < QUADS
    first, second = [jnp.where(half, u_ref[pl.ds(i, 8, stride=steps), :], 0.0) for i in range(2)]
    for m, rate in enumerate(mode_rows(rate_ref)):
        late = jnp.exp(-float(steps - 1) * rate) * first + jnp.exp(-float(steps - 2) * rate) * second
        end_ref[m * 8 : m * 8 + 8, :] = end_ref[m * 8 : m * 8 + 8, :] + late


def block_states(end_ref, rate_ref, state_ref, steps):
    for m in range(MODES):
        x = end_ref[m * 8 : m * 8 + 8, :]
        rate = rate_ref[m * 8 : m * 8 + 4, :]
        state = jnp.exp(-float(steps) * rate) * x[0:4] + x[4:8]
        put_rows(state_ref, m, state)


def put_rows(ref, m, value):
    height = ref.shape[1]
    if height <= QUADS:
        for i in range(QUADS // height):
            ref[m * (QUADS // height) + i] = value[i * height : (i + 1) * height]
    else:
        each = height // QUADS
        ref[m // each, (m % each) * QUADS : (m % each + 1) * QUADS, :] = value


def get_rows(ref, m):
    height = ref.shape[1]
    if height <= QUADS:
        n = QUADS // height
        return jnp.concatenate([ref[m * n + i] for i in range(n)], axis=0)
    each = height // QUADS
    return ref[m // each, (m % each) * QUADS : (m % each + 1) * QUADS, :]


def local_outputs(x, begin, end, u_ref, rate_ref, gain_ref, skip_ref, y_ref, steps):
    decay = [jnp.exp(-x) for x in mode_rows(rate_ref)]
    gain = mode_rows(gain_ref)
    skip = skip_ref[...]

    def step(t, x):
        u = u_ref[pl.ds(t, 8, stride=steps), :]
        x = tuple(d * a + u for d, a in zip(decay, x))
        y_ref[pl.ds(t, 8, stride=steps), :] = total([g * a for g, a in zip(gain, x)] + [skip * u])
        return x

    return lax.fori_loop(begin, end, step, x, unroll=4)


def total(parts):
    while len(parts) > 1:
        parts = [sum(parts[i : i + 2]) for i in range(0, len(parts), 2)]
    return parts[0]


def carried(end_ref, carry_ref, rate_ref, gain_ref, base_ref, steps):
    for m in range(MODES):
        carry = get_rows(carry_ref, m)
        rate = rate_ref[m * 8 : m * 8 + 4, :]
        later = end_ref[m * 8 : m * 8 + 4, :] + jnp.exp(-float(steps) * rate) * carry
        both = jnp.concatenate([carry, later], axis=0)
        base_ref[m * 8 : m * 8 + 8, :] = gain_ref[m * 8 : m * 8 + 8, :] * both


def add_carried(i, rows, base_ref, rate_ref, y_ref, steps):
    rate = mode_rows(rate_ref)
    decay = [jnp.exp(-x) for x in rate]
    begin = i * rows
    past = begin.astype(jnp.float32)
    state = tuple(a * jnp.exp(-past * r) for a, r in zip(mode_rows(base_ref), rate))

    def step(t, state):
        state = tuple(d * a for d, a in zip(decay, state))
        at = pl.ds(begin + t, 8, stride=steps)
        y_ref[at, :] = y_ref[at, :] + total(list(state))
        return state

    lax.fori_loop(0, rows, step, state, unroll=8)


def gathered(y_ref, out_ref, p, h, t, rows, steps):
    for q in range(QUADS):
        at = pl.multiple_of((h * QUADS + q) * steps + t, 32)
        out_ref[p, :, q * LANES : (q + 1) * LANES] = y_ref[pl.ds(at, rows), :].astype(jnp.bfloat16)


def kernel(
    doc_hbm, feat_hbm, short_hbm, residues_hbm, rates_hbm, skip_hbm,
    out_ref,
    doc_ref, feat_ref, short_ref, residues_ref, rates_ref, skipin_ref,
    rim_ref, rimin_ref, modes_ref, gate_ref, prod_ref, recv_ref, edge_ref, final_ref, cross_ref, edgewide_ref,
    u_ref, y_ref, mixed_ref, back_ref,
    rate_ref, gain_ref, skip_ref, end_ref, base_ref, state_ref, packed_ref, states_ref, carries_ref, carry_ref, fade_ref,
    load, pair_send, pair_recv, cross_send, there_send, there_recv, edge_send, back_send, back_recv,
    ring_send, ring_recv, near_send, near_recv,
):
    seqs, chans = lax.axis_size("seq"), lax.axis_size("chan")
    seq, chan = lax.axis_index("seq"), lax.axis_index("chan")
    peers, rows = prod_ref.shape[0], feat_ref.shape[1]
    blocks = 2 * seqs
    owners = state_ref.shape[0]
    steps = peers * rows // 2
    z, plane = chan // peers, chan % peers
    block = seq * 2 + z
    me = seq * chans + chan
    count = seqs * chans
    after, prior = (me + 1) % count, (me + count - 1) % count

    def in_plane(p):
        return (seq, z * peers + p)

    def in_column(b):
        return (b // 2, (b % 2) * peers + plane)

    def of_all(i):
        return (i // chans, i % chans)

    def remote(src, dst, send, recv, device):
        return pltpu.make_async_remote_copy(src, dst, send, recv, device_id=device, device_id_type=MESH)

    barrier = pltpu.get_barrier_semaphore()

    def greet(device):
        pl.semaphore_signal(barrier, inc=1, device_id=device, device_id_type=MESH)

    pairs = (
        (feat_hbm.at[pl.ds(1, 2)], feat_ref.at[pl.ds(1, 2)]), (short_hbm, short_ref),
        (doc_hbm, doc_ref), (rates_hbm, rates_ref), (residues_hbm, residues_ref), (skip_hbm, skipin_ref),
        (feat_hbm.at[0], feat_ref.at[0]),
    )
    loads = [pltpu.make_async_copy(src, dst, load.at[i]) for i, (src, dst) in enumerate(pairs)]
    for copy in loads:
        copy.start()

    @pl.loop(1, blocks)
    def _(k):
        greet(in_column((block + k) % blocks))

    greet(of_all(prior))

    @pl.loop(1, peers)
    def _(k):
        greet(in_plane((plane + k) % peers))

    for copy in loads[2:6]:
        copy.wait()
    rates = rates_ref[...]
    modes_ref[z, 0:MODES, :] = rates
    modes_ref[z, MODES : 2 * MODES, :] = mode_gain(rates, residues_ref[...])
    modes_ref[z, 2 * MODES : 2 * MODES + 8, :] = jnp.broadcast_to(skipin_ref[...], (8, HALF))
    one, two = tap_masks(me * rows, doc_ref, rows)
    for copy in loads[:2]:
        copy.wait()

    @pl.loop(0, peers)
    def _(p):
        for half in range(2):
            edges = form_edges(half * peers + p, feat_ref)
            edge_ref[p, :, half * HALF : (half + 1) * HALF] = edges
            prod_ref[p, rows : rows + EDGES, half * HALF : (half + 1) * HALF] = edges

    def make(k):
        p = (plane + k) % peers
        for half in range(2):
            value = form_product(half * peers + p, one, two, feat_ref, short_ref)
            prod_ref[p, 0:rows, half * HALF : (half + 1) * HALF] = value

    soon = peers // 2
    pl.loop(1, soon)(make)
    loads[6].wait()
    rim_ref[...] = feat_ref[0, rows - 2 : rows, :]

    pl.semaphore_wait(barrier, peers + blocks - 1)

    partner = (seq, (1 - z) * peers + plane)

    def params(slot, part):
        at = modes_ref.at[slot, pl.ds(0, MODES)] if part == 0 else modes_ref.at[slot, pl.ds(MODES, MODES + 8)]
        return remote(at, at, pair_send.at[part], pair_recv.at[part], partner)

    params(z, 0).start()

    last = peers - 1

    def edges_there(p):
        return remote(edge_ref.at[p], final_ref, edge_send.at[p], pair_recv.at[4], in_plane(p))

    def there(p, slot):
        return remote(prod_ref.at[p], recv_ref.at[slot], there_send.at[p], there_recv.at[slot], in_plane(p))

    @pl.when(plane == last)
    def _():
        @pl.loop(0, last)
        def _(p):
            edges_there(p).start()

        final_ref[...] = edge_ref[last]

    def send(k):
        there((plane + k) % peers, plane).start()

    early = min(6, soon)
    pl.loop(1, early)(send)
    pl.loop(soon, peers + 1)(make)
    middle = max(early, peers - 4)
    pl.loop(early, middle)(send)

    @pl.when(plane != last)
    def _():
        edges_there(plane).wait_recv()

    def cross():
        ahead = in_column((block + 1) % blocks)
        return remote(final_ref, cross_ref, cross_send, pair_recv.at[3], ahead)

    cross().start()
    pl.loop(middle, peers)(send)
    rim = remote(rim_ref, rimin_ref, pair_send.at[2], pair_recv.at[2], of_all(after))
    rim.start()
    params(z, 1).start()

    @pl.loop(0, 2 * peers)
    def _(i):
        form_gate(i, one, two, feat_ref, short_ref, gate_ref)

    def widen(slot, value):
        for q in range(QUADS):
            at = pl.multiple_of((q * (peers + 1) + slot) * 8, 8)
            edgewide_ref[pl.ds(at, 8), :] = value[:, q * LANES : (q + 1) * LANES].astype(jnp.float32)

    def take(p, source):
        spread(p, source, u_ref)
        widen(p + 1, source[p, rows : rows + EDGES, :])

    take(plane, prod_ref)

    @pl.loop(1, peers)
    def _(k):
        p = (plane + peers - k) % peers
        there(plane, p).wait_recv()
        take(p, recv_ref)

    params(1 - z, 0).wait_recv()
    scatter_rates(modes_ref, rate_ref)
    widen(0, jnp.zeros_like(cross_ref))
    repair(block * peers * rows, rows, plane, doc_ref, short_ref, edgewide_ref, u_ref)
    for q in range(QUADS):
        u_ref[q * steps : q * steps + 2, :] = jnp.zeros((2, LANES), jnp.float32)
    local_states(u_ref, rate_ref, end_ref, steps)
    cross().wait_recv()
    widen(0, cross_ref[...])
    repair(block * peers * rows, rows, plane, doc_ref, short_ref, edgewide_ref, u_ref)
    add_first(u_ref, rate_ref, end_ref, steps)
    block_states(end_ref, rate_ref, state_ref, steps)
    packed_ref[...] = state_ref[...].astype(jnp.bfloat16)

    def owned(b):
        return (b // 2) % owners

    def state_copy(b, slot):
        return remote(packed_ref.at[owned(b)], states_ref.at[slot], ring_send.at[b], ring_recv.at[slot], in_column(b))

    @pl.loop(1, blocks)
    def _(k):
        state_copy((block + k) % blocks, block).start()

    states_ref[block] = packed_ref[owned(block)]
    params(1 - z, 1).wait_recv()
    scatter_gains(modes_ref, gain_ref, skip_ref)
    for m in range(MODES):
        put_rows(fade_ref, m, jnp.exp(-2.0 * steps * rate_ref[m * 8 : m * 8 + 4, :]))
    zero = (jnp.zeros((8, LANES), jnp.float32),) * MODES
    local_outputs(zero, 0, steps, u_ref, rate_ref, gain_ref, skip_ref, y_ref, steps)
    @pl.loop(1, blocks)
    def _(k):
        state_copy(block, (block + k) % blocks).wait_recv()

    fade = fade_ref[owned(block)]

    def chain(b, carry):
        carries_ref[b] = carry
        return fade * carry + states_ref[b].astype(jnp.float32)

    lax.fori_loop(0, blocks, chain, jnp.zeros_like(fade))
    group = seq // owners * owners

    def near(j):
        return group + (owned(block) + j) % owners

    def carry_copy(to, slot):
        return remote(
            carries_ref.at[to * 2 + z], carry_ref.at[slot], near_send.at[to % owners], near_recv.at[slot],
            (to, chan),
        )

    @pl.loop(1, owners)
    def _(j):
        carry_copy(near(j), owned(block)).start()

    carry_ref[owned(block)] = carries_ref[block]
    rim.wait_recv()

    @pl.loop(0, 2 * peers)
    def _(i):
        repair_gate(i, one, two, feat_ref, rimin_ref, short_ref, gate_ref)

    @pl.loop(1, owners)
    def _(j):
        carry_copy(seq, near(j) % owners).wait_recv()

    carried(end_ref, carry_ref, rate_ref, gain_ref, base_ref, steps)

    def back(p, slot):
        return remote(mixed_ref.at[p], back_ref.at[slot], back_send.at[p], back_recv.at[slot], in_plane(p))

    @pl.loop(0, peers // 2)
    def _(k):
        i = (plane + k) % (peers // 2)
        add_carried(i, rows, base_ref, rate_ref, y_ref, steps)
        for h in range(2):
            p = h * (peers // 2) + i
            gathered(y_ref, mixed_ref, p, h, i * rows, rows, steps)

            @pl.when(p != plane)
            def _():
                back(p, plane).start()

    def finish(p, source):
        for half in range(2):
            cols = pl.ds(pl.multiple_of((half * peers + p) * HALF, HALF), HALF)
            value = source[p, :, half * HALF : (half + 1) * HALF].astype(jnp.float32)
            out_ref[:, cols] = (gate_ref[:, cols].astype(jnp.float32) * value).astype(jnp.bfloat16)

    finish(plane, mixed_ref)

    @pl.loop(1, peers)
    def _(k):
        p = (plane + k) % peers
        back(plane, p).wait_recv()
        finish(p, back_ref)

    rim.wait_send()
    params(z, 0).wait_send()
    params(z, 1).wait_send()

    cross().wait_send()

    @pl.when(plane == last)
    def _():
        @pl.loop(0, last)
        def _(p):
            edges_there(p).wait_send()

    @pl.loop(1, peers)
    def _(k):
        p = (plane + k) % peers
        there(p, plane).wait_send()
        back(p, plane).wait_send()

    @pl.loop(1, blocks)
    def _(k):
        state_copy((block + k) % blocks, block).wait_send()

    @pl.loop(1, owners)
    def _(j):
        carry_copy(near(j), owned(block)).wait_send()


def per_device(features, short_weights, doc_lengths, residues, rates, skip):
    seqs = lax.axis_size("seq")
    blocks = 2 * seqs
    owners = min(8, seqs)
    peers = lax.axis_size("chan") // 2
    rows, width = features.shape[1:]
    bf16, f32 = jnp.bfloat16, jnp.float32
    vmem = pltpu.VMEM
    operands = (doc_lengths[None, :], features, short_weights, residues, rates, skip[None, :])
    wide = vmem((peers * rows * QUADS, LANES), f32)
    table = vmem((8 * MODES, LANES), f32)
    rim = vmem((2, width), bf16)
    moved = vmem((peers, rows, 2 * HALF), bf16)
    sent = vmem((peers, rows + EDGES, 2 * HALF), bf16)
    edges = vmem((peers, EDGES, 2 * HALF), bf16)
    edge = vmem((EDGES, 2 * HALF), bf16)
    height = MODES * QUADS // owners
    owned = vmem((owners, height, LANES), f32)
    dma = lambda *n: pltpu.SemaphoreType.DMA(n)
    return pl.pallas_call(
        kernel,
        out_shape=pltpu.VMEM((rows, width), bf16),
        in_specs=[pl.BlockSpec(memory_space=pl.ANY)] * 6,
        out_specs=VMEM,
        scratch_shapes=[vmem(x.shape, x.dtype) for x in operands]
        + [
            rim, rim,
            vmem((2, 2 * MODES + 8, HALF), f32),
            vmem((rows, width), bf16),
            sent, sent, edges, edge, edge, vmem((8 * QUADS * (peers + 1), LANES), f32),
            wide, wide, moved, moved,
            table, table, vmem((8, LANES), f32), table, table,
            owned, vmem((owners, height, LANES), bf16), vmem((blocks, height, LANES), bf16),
            vmem((blocks, height, LANES), f32), owned, owned,
            dma(7), dma(3), dma(5), pltpu.SemaphoreType.DMA, dma(peers), dma(peers), dma(peers), dma(peers), dma(peers),
            dma(blocks), dma(blocks), dma(owners), dma(owners),
        ],
        compiler_params=pltpu.CompilerParams(
            collective_id=0, has_side_effects=True, vmem_limit_bytes=58 * 2**20
        ),
    )(*operands)


def solution(mesh):
    placed = (P(None, ("seq", "chan"), None), P(), P(), P(None, "chan"), P(None, "chan"), P("chan"))
    return jax.shard_map(
        per_device, mesh=mesh, in_specs=placed, out_specs=P(("seq", "chan"), None), check_vma=False
    )
```

```python
import jax
import jax.numpy as jnp
from jax import lax
from jax.experimental import pallas as pl
from jax.experimental.pallas import tpu as pltpu
from jax.sharding import PartitionSpec as P

MODES = 16
EDGES = 8
LANES = 128
QUADS = 4
HALF = 256
VMEM = pl.BlockSpec(memory_space=pltpu.VMEM)
MESH = pl.DeviceIdType.MESH


def doc_starts(doc_ref):
    n = doc_ref.shape[1]
    lengths = doc_ref[...].astype(jnp.float32)
    rows = lax.broadcasted_iota(jnp.int32, (n, n), 0)
    cols = lax.broadcasted_iota(jnp.int32, (n, n), 1)
    wide = jnp.broadcast_to(lengths, (n, n))
    column = jnp.sum(jnp.where(rows == cols, wide, 0.0), axis=1, keepdims=True)
    return jnp.sum(jnp.where(rows < cols, column, 0.0), axis=0, keepdims=True)


def tap_masks(first, doc_ref, rows):
    starts = doc_starts(doc_ref)
    n = starts.shape[1]
    index = lax.broadcasted_iota(jnp.int32, (rows, n), 0)
    position = (first + index).astype(jnp.float32)
    here = jnp.max(jnp.where(starts == position, 1.0, 0.0), axis=1, keepdims=True)
    before = jnp.max(jnp.where(starts == position - 1.0, 1.0, 0.0), axis=1, keepdims=True)
    one = jnp.broadcast_to(here, (rows, HALF)) < 0.5
    two = jnp.broadcast_to(here + before, (rows, HALF)) < 0.5
    return one, two


def filtered(x, x1, x2, one, two, short_ref, s, cols):
    return (
        x * short_ref[s, 0:1, cols]
        + jnp.where(one, x1, 0.0) * short_ref[s, 1:2, cols]
        + jnp.where(two, x2, 0.0) * short_ref[s, 2:3, cols]
    )


def form_product(block, one, two, feat_ref, short_ref):
    cols = pl.ds(pl.multiple_of(block * HALF, HALF), HALF)
    streams = []
    for s in (1, 2):
        x = feat_ref[s, :, cols].astype(jnp.float32)
        streams.append(
            filtered(x, pltpu.roll(x, 1, 0), pltpu.roll(x, 2, 0), one, two, short_ref, s, cols)
        )
    return (streams[0] * streams[1]).astype(jnp.bfloat16)


def form_edges(block, feat_ref):
    rows = feat_ref.shape[1]
    cols = pl.ds(pl.multiple_of(block * HALF, HALF), HALF)
    row = lax.broadcasted_iota(jnp.int32, (8, HALF), 0)
    (key_top, key_end), (value_top, value_end) = [
        (
            feat_ref[s, 0:16, cols].astype(jnp.float32)[0:8],
            feat_ref[s, rows - 16 : rows, cols].astype(jnp.float32)[8:16],
        )
        for s in (1, 2)
    ]
    lower = jnp.where(row < 6, pltpu.roll(value_end, 6, 0), key_end)
    upper = jnp.where(row < 2, key_top, pltpu.roll(value_top, 2, 0))
    return jnp.where(row < 4, upper, lower).astype(jnp.bfloat16)


def form_gate(block, one, two, feat_ref, short_ref, gate_ref):
    cols = pl.ds(pl.multiple_of(block * HALF, HALF), HALF)
    x = feat_ref[0, :, cols].astype(jnp.float32)
    gate = filtered(x, pltpu.roll(x, 1, 0), pltpu.roll(x, 2, 0), one, two, short_ref, 0, cols)
    gate_ref[:, cols] = gate.astype(jnp.bfloat16)


def repair_gate(block, one, two, feat_ref, rim_ref, short_ref, gate_ref):
    row = lax.broadcasted_iota(jnp.int32, (16, HALF), 0)
    cols = pl.ds(pl.multiple_of(block * HALF, HALF), HALF)
    x = feat_ref[0, 0:16, cols].astype(jnp.float32)
    rim = rim_ref[:, cols].astype(jnp.float32)
    x1 = jnp.where(row == 0, rim[1:2], pltpu.roll(x, 1, 0))
    x2 = jnp.where(row == 0, rim[0:1], jnp.where(row == 1, rim[1:2], pltpu.roll(x, 2, 0)))
    gate = filtered(x, x1, x2, one[0:16], two[0:16], short_ref, 0, cols)
    gate_ref[0:16, cols] = gate.astype(jnp.bfloat16)


def repair(first, rows, plane, doc_ref, short_ref, edge_ref, u_ref):
    peers = edge_ref.shape[0] // (8 * QUADS) - 1
    steps = peers * rows // 2
    starts = doc_starts(doc_ref)
    n = starts.shape[1]
    index = lax.broadcasted_iota(jnp.int32, (peers, n), 0)
    position = (first + index * rows).astype(jnp.float32)

    def begins(shift):
        hit = jnp.where(starts == position + shift, 1.0, 0.0)
        return jnp.broadcast_to(jnp.max(hit, axis=1, keepdims=True), (peers, HALF))

    before, here, later = begins(-1.0), begins(0.0), begins(1.0)
    one = (here < 0.5, later < 0.5)
    two = (here + before < 0.5, later + here < 0.5)
    for half in range(2):
        cols = pl.ds(pl.multiple_of((half * peers + plane) * HALF, HALF), HALF)
        lanes = slice(half * HALF, (half + 1) * HALF)

        def edge(slot, r):
            parts = [
                edge_ref[pl.ds((half * 2 + i) * 8 * (peers + 1) + slot * 8 + r, peers, stride=8), :]
                for i in range(HALF // LANES)
            ]
            return jnp.concatenate(parts, axis=1)

        fixed = []
        for s, top, last in ((1, 0, 6), (2, 2, 4)):
            x = [edge(0, last), edge(0, last + 1), edge(1, top), edge(1, top + 1)]
            fixed.append(
                [
                    filtered(x[2 + i], x[1 + i], x[i], one[i], two[i], short_ref, s, cols)
                    for i in range(2)
                ]
            )
        for i in range(2):
            value = (fixed[0][i] * fixed[1][i]).astype(jnp.bfloat16).astype(jnp.float32)
            for h in range(2):
                for j in range(HALF // LANES):
                    q = half * (HALF // LANES) + j
                    at = pl.ds((h * QUADS + q) * steps + i, peers // 2, stride=rows)
                    u_ref[at, :] = value[h * (peers // 2) : (h + 1) * (peers // 2), j * LANES : (j + 1) * LANES]


def mode_gain(rate, residue):
    x = 2.0 * rate
    series = jnp.ones_like(x)
    for n in range(9, 1, -1):
        series = 1.0 - x * (1.0 / n) * series
    return residue * jnp.sqrt(x * series)


def scatter_rates(modes_ref, rate_ref):
    for q in range(QUADS):
        cols = slice((q % 2) * LANES, (q % 2 + 1) * LANES)
        for h in range(2):
            rate_ref[pl.ds(h * QUADS + q, MODES, stride=8), :] = modes_ref[q // 2, 0:MODES, cols]


def scatter_gains(modes_ref, gain_ref, skip_ref):
    for q in range(QUADS):
        cols = slice((q % 2) * LANES, (q % 2 + 1) * LANES)
        for h in range(2):
            at = h * QUADS + q
            gain_ref[pl.ds(at, MODES, stride=8), :] = modes_ref[q // 2, MODES : 2 * MODES, cols]
            skip_ref[at : at + 1, :] = modes_ref[q // 2, 2 * MODES : 2 * MODES + 1, cols]


def spread(p, recv_ref, u_ref):
    peers, height, _ = recv_ref.shape
    rows = height - EDGES
    steps = peers * rows // 2
    h = p // (peers // 2)
    t = (p % (peers // 2)) * rows
    for q in range(QUADS):
        at = pl.multiple_of((h * QUADS + q) * steps + t, 32)
        u_ref[pl.ds(at, rows), :] = recv_ref[p, 0:rows, q * LANES : (q + 1) * LANES].astype(jnp.float32)


def mode_rows(ref):
    return [ref[m * 8 : m * 8 + 8, :] for m in range(MODES)]


def local_states(u_ref, rate_ref, end_ref, steps):
    decay = [jnp.exp(-x) for x in mode_rows(rate_ref)]

    def step(t, x):
        u = u_ref[pl.ds(t, 8, stride=steps), :]
        return tuple(d * a + u for d, a in zip(decay, x))

    zero = jnp.zeros((8, LANES), jnp.float32)
    x = lax.fori_loop(0, steps, step, (zero,) * MODES, unroll=8)
    for m in range(MODES):
        end_ref[m * 8 : m * 8 + 8, :] = x[m]


def add_first(u_ref, rate_ref, end_ref, steps):
    half = lax.broadcasted_iota(jnp.int32, (8, LANES), 0) < QUADS
    first, second = [jnp.where(half, u_ref[pl.ds(i, 8, stride=steps), :], 0.0) for i in range(2)]
    for m, rate in enumerate(mode_rows(rate_ref)):
        late = jnp.exp(-float(steps - 1) * rate) * first + jnp.exp(-float(steps - 2) * rate) * second
        end_ref[m * 8 : m * 8 + 8, :] = end_ref[m * 8 : m * 8 + 8, :] + late


def block_states(end_ref, rate_ref, state_ref, steps):
    for m in range(MODES):
        x = end_ref[m * 8 : m * 8 + 8, :]
        rate = rate_ref[m * 8 : m * 8 + 4, :]
        state = jnp.exp(-float(steps) * rate) * x[0:4] + x[4:8]
        put_rows(state_ref, m, state)


def put_rows(ref, m, value):
    height = ref.shape[1]
    if height <= QUADS:
        for i in range(QUADS // height):
            ref[m * (QUADS // height) + i] = value[i * height : (i + 1) * height]
    else:
        each = height // QUADS
        ref[m // each, (m % each) * QUADS : (m % each + 1) * QUADS, :] = value


def get_rows(ref, m):
    height = ref.shape[1]
    if height <= QUADS:
        n = QUADS // height
        return jnp.concatenate([ref[m * n + i] for i in range(n)], axis=0)
    each = height // QUADS
    return ref[m // each, (m % each) * QUADS : (m % each + 1) * QUADS, :]


def local_outputs(x, begin, end, u_ref, rate_ref, gain_ref, skip_ref, y_ref, steps):
    decay = [jnp.exp(-x) for x in mode_rows(rate_ref)]
    gain = mode_rows(gain_ref)
    skip = skip_ref[...]

    def step(t, x):
        u = u_ref[pl.ds(t, 8, stride=steps), :]
        x = tuple(d * a + u for d, a in zip(decay, x))
        y_ref[pl.ds(t, 8, stride=steps), :] = total([g * a for g, a in zip(gain, x)] + [skip * u])
        return x

    return lax.fori_loop(begin, end, step, x, unroll=4)


def total(parts):
    while len(parts) > 1:
        parts = [sum(parts[i : i + 2]) for i in range(0, len(parts), 2)]
    return parts[0]


def carried(end_ref, carry_ref, rate_ref, gain_ref, base_ref, steps):
    for m in range(MODES):
        carry = get_rows(carry_ref, m)
        rate = rate_ref[m * 8 : m * 8 + 4, :]
        later = end_ref[m * 8 : m * 8 + 4, :] + jnp.exp(-float(steps) * rate) * carry
        both = jnp.concatenate([carry, later], axis=0)
        base_ref[m * 8 : m * 8 + 8, :] = gain_ref[m * 8 : m * 8 + 8, :] * both


def add_carried(i, rows, base_ref, rate_ref, y_ref, steps):
    rate = mode_rows(rate_ref)
    decay = [jnp.exp(-x) for x in rate]
    begin = i * rows
    past = begin.astype(jnp.float32)
    state = tuple(a * jnp.exp(-past * r) for a, r in zip(mode_rows(base_ref), rate))

    def step(t, state):
        state = tuple(d * a for d, a in zip(decay, state))
        at = pl.ds(begin + t, 8, stride=steps)
        y_ref[at, :] = y_ref[at, :] + total(list(state))
        return state

    lax.fori_loop(0, rows, step, state, unroll=8)


def gathered(y_ref, out_ref, p, h, t, rows, steps):
    for q in range(QUADS):
        at = pl.multiple_of((h * QUADS + q) * steps + t, 32)
        out_ref[p, :, q * LANES : (q + 1) * LANES] = y_ref[pl.ds(at, rows), :].astype(jnp.bfloat16)


def kernel(
    doc_hbm, feat_hbm, short_hbm, residues_hbm, rates_hbm, skip_hbm,
    out_ref,
    doc_ref, feat_ref, short_ref, residues_ref, rates_ref, skipin_ref,
    rim_ref, rimin_ref, modes_ref, gate_ref, prod_ref, recv_ref, edge_ref, final_ref, cross_ref, edgewide_ref,
    u_ref, y_ref, mixed_ref, back_ref,
    rate_ref, gain_ref, skip_ref, end_ref, base_ref, state_ref, packed_ref, states_ref, carries_ref, carry_ref, fade_ref,
    load, pair_send, pair_recv, cross_send, there_send, there_recv, edge_send, back_send, back_recv,
    ring_send, ring_recv, near_send, near_recv,
):
    seqs, chans = lax.axis_size("seq"), lax.axis_size("chan")
    seq, chan = lax.axis_index("seq"), lax.axis_index("chan")
    peers, rows = prod_ref.shape[0], feat_ref.shape[1]
    blocks = 2 * seqs
    owners = state_ref.shape[0]
    steps = peers * rows // 2
    z, plane = chan // peers, chan % peers
    block = seq * 2 + z
    me = seq * chans + chan
    count = seqs * chans
    after, prior = (me + 1) % count, (me + count - 1) % count

    def in_plane(p):
        return (seq, z * peers + p)

    def in_column(b):
        return (b // 2, (b % 2) * peers + plane)

    def of_all(i):
        return (i // chans, i % chans)

    def remote(src, dst, send, recv, device):
        return pltpu.make_async_remote_copy(src, dst, send, recv, device_id=device, device_id_type=MESH)

    barrier = pltpu.get_barrier_semaphore()

    def greet(device):
        pl.semaphore_signal(barrier, inc=1, device_id=device, device_id_type=MESH)

    pairs = (
        (feat_hbm.at[pl.ds(1, 2)], feat_ref.at[pl.ds(1, 2)]), (short_hbm, short_ref),
        (doc_hbm, doc_ref), (rates_hbm, rates_ref), (residues_hbm, residues_ref), (skip_hbm, skipin_ref),
        (feat_hbm.at[0], feat_ref.at[0]),
    )
    loads = [pltpu.make_async_copy(src, dst, load.at[i]) for i, (src, dst) in enumerate(pairs)]
    for copy in loads:
        copy.start()

    @pl.loop(1, blocks)
    def _(k):
        greet(in_column((block + k) % blocks))

    greet(of_all(prior))

    @pl.loop(1, peers)
    def _(k):
        greet(in_plane((plane + k) % peers))

    for copy in loads[2:6]:
        copy.wait()
    rates = rates_ref[...]
    modes_ref[z, 0:MODES, :] = rates
    modes_ref[z, MODES : 2 * MODES, :] = mode_gain(rates, residues_ref[...])
    modes_ref[z, 2 * MODES : 2 * MODES + 8, :] = jnp.broadcast_to(skipin_ref[...], (8, HALF))
    one, two = tap_masks(me * rows, doc_ref, rows)
    for copy in loads[:2]:
        copy.wait()

    @pl.loop(0, peers)
    def _(p):
        for half in range(2):
            edges = form_edges(half * peers + p, feat_ref)
            edge_ref[p, :, half * HALF : (half + 1) * HALF] = edges
            prod_ref[p, rows : rows + EDGES, half * HALF : (half + 1) * HALF] = edges

    def make(k):
        p = (plane + k) % peers
        for half in range(2):
            value = form_product(half * peers + p, one, two, feat_ref, short_ref)
            prod_ref[p, 0:rows, half * HALF : (half + 1) * HALF] = value

    soon = peers // 2
    pl.loop(1, soon)(make)
    loads[6].wait()
    rim_ref[...] = feat_ref[0, rows - 2 : rows, :]

    pl.semaphore_wait(barrier, peers + blocks - 1)

    partner = (seq, (1 - z) * peers + plane)

    def params(slot, part):
        at = modes_ref.at[slot, pl.ds(0, MODES)] if part == 0 else modes_ref.at[slot, pl.ds(MODES, MODES + 8)]
        return remote(at, at, pair_send.at[part], pair_recv.at[part], partner)

    params(z, 0).start()

    last = peers - 1

    def edges_there(p):
        return remote(edge_ref.at[p], final_ref, edge_send.at[p], pair_recv.at[4], in_plane(p))

    def there(p, slot):
        return remote(prod_ref.at[p], recv_ref.at[slot], there_send.at[p], there_recv.at[slot], in_plane(p))

    @pl.when(plane == last)
    def _():
        @pl.loop(0, last)
        def _(p):
            edges_there(p).start()

        final_ref[...] = edge_ref[last]

    def send(k):
        there((plane + k) % peers, plane).start()

    early = min(6, soon)
    pl.loop(1, early)(send)
    pl.loop(soon, peers + 1)(make)
    middle = max(early, peers - 4)
    pl.loop(early, middle)(send)

    @pl.when(plane != last)
    def _():
        edges_there(plane).wait_recv()

    def cross():
        ahead = in_column((block + 1) % blocks)
        return remote(final_ref, cross_ref, cross_send, pair_recv.at[3], ahead)

    cross().start()
    pl.loop(middle, peers)(send)
    rim = remote(rim_ref, rimin_ref, pair_send.at[2], pair_recv.at[2], of_all(after))
    rim.start()
    params(z, 1).start()

    @pl.loop(0, 2 * peers)
    def _(i):
        form_gate(i, one, two, feat_ref, short_ref, gate_ref)

    def widen(slot, value):
        for q in range(QUADS):
            at = pl.multiple_of((q * (peers + 1) + slot) * 8, 8)
            edgewide_ref[pl.ds(at, 8), :] = value[:, q * LANES : (q + 1) * LANES].astype(jnp.float32)

    def take(p, source):
        spread(p, source, u_ref)
        widen(p + 1, source[p, rows : rows + EDGES, :])

    take(plane, prod_ref)

    @pl.loop(1, peers)
    def _(k):
        p = (plane + peers - k) % peers
        there(plane, p).wait_recv()
        take(p, recv_ref)

    params(1 - z, 0).wait_recv()
    scatter_rates(modes_ref, rate_ref)
    widen(0, jnp.zeros_like(cross_ref))
    repair(block * peers * rows, rows, plane, doc_ref, short_ref, edgewide_ref, u_ref)
    for q in range(QUADS):
        u_ref[q * steps : q * steps + 2, :] = jnp.zeros((2, LANES), jnp.float32)
    local_states(u_ref, rate_ref, end_ref, steps)
    cross().wait_recv()
    widen(0, cross_ref[...])
    repair(block * peers * rows, rows, plane, doc_ref, short_ref, edgewide_ref, u_ref)
    add_first(u_ref, rate_ref, end_ref, steps)
    block_states(end_ref, rate_ref, state_ref, steps)
    packed_ref[...] = state_ref[...].astype(jnp.bfloat16)

    def owned(b):
        return (b // 2) % owners

    def state_copy(b, slot):
        return remote(packed_ref.at[owned(b)], states_ref.at[slot], ring_send.at[b], ring_recv.at[slot], in_column(b))

    @pl.loop(1, blocks)
    def _(k):
        state_copy((block + k) % blocks, block).start()

    states_ref[block] = packed_ref[owned(block)]
    params(1 - z, 1).wait_recv()
    scatter_gains(modes_ref, gain_ref, skip_ref)
    for m in range(MODES):
        put_rows(fade_ref, m, jnp.exp(-2.0 * steps * rate_ref[m * 8 : m * 8 + 4, :]))
    zero = (jnp.zeros((8, LANES), jnp.float32),) * MODES
    local_outputs(zero, 0, steps, u_ref, rate_ref, gain_ref, skip_ref, y_ref, steps)
    @pl.loop(1, blocks)
    def _(k):
        state_copy(block, (block + k) % blocks).wait_recv()

    fade = fade_ref[owned(block)]

    def chain(b, carry):
        carries_ref[b] = carry
        return fade * carry + states_ref[b].astype(jnp.float32)

    lax.fori_loop(0, blocks, chain, jnp.zeros_like(fade))
    group = seq // owners * owners

    def near(j):
        return group + (owned(block) + j) % owners

    def carry_copy(to, slot):
        return remote(
            carries_ref.at[to * 2 + z], carry_ref.at[slot], near_send.at[to % owners], near_recv.at[slot],
            (to, chan),
        )

    @pl.loop(1, owners)
    def _(j):
        carry_copy(near(j), owned(block)).start()

    carry_ref[owned(block)] = carries_ref[block]
    rim.wait_recv()

    @pl.loop(0, 2 * peers)
    def _(i):
        repair_gate(i, one, two, feat_ref, rimin_ref, short_ref, gate_ref)

    @pl.loop(1, owners)
    def _(j):
        carry_copy(seq, near(j) % owners).wait_recv()

    carried(end_ref, carry_ref, rate_ref, gain_ref, base_ref, steps)

    def back(p, slot):
        return remote(mixed_ref.at[p], back_ref.at[slot], back_send.at[p], back_recv.at[slot], in_plane(p))

    @pl.loop(0, peers // 2)
    def _(k):
        i = (plane + k) % (peers // 2)
        add_carried(i, rows, base_ref, rate_ref, y_ref, steps)
        for h in range(2):
            p = h * (peers // 2) + i
            gathered(y_ref, mixed_ref, p, h, i * rows, rows, steps)

            @pl.when(p != plane)
            def _():
                back(p, plane).start()

    def finish(p, source):
        for half in range(2):
            cols = pl.ds(pl.multiple_of((half * peers + p) * HALF, HALF), HALF)
            value = source[p, :, half * HALF : (half + 1) * HALF].astype(jnp.float32)
            out_ref[:, cols] = (gate_ref[:, cols].astype(jnp.float32) * value).astype(jnp.bfloat16)

    finish(plane, mixed_ref)

    @pl.loop(0, peers)
    def _(k):
        p = (plane + peers - k // 2) % (peers // 2) + k % 2 * (peers // 2)

        @pl.when(p != plane)
        def _():
            back(plane, p).wait_recv()
            finish(p, back_ref)

    rim.wait_send()
    params(z, 0).wait_send()
    params(z, 1).wait_send()

    cross().wait_send()

    @pl.when(plane == last)
    def _():
        @pl.loop(0, last)
        def _(p):
            edges_there(p).wait_send()

    @pl.loop(1, peers)
    def _(k):
        p = (plane + k) % peers
        there(p, plane).wait_send()
        back(p, plane).wait_send()

    @pl.loop(1, blocks)
    def _(k):
        state_copy((block + k) % blocks, block).wait_send()

    @pl.loop(1, owners)
    def _(j):
        carry_copy(near(j), owned(block)).wait_send()


def per_device(features, short_weights, doc_lengths, residues, rates, skip):
    seqs = lax.axis_size("seq")
    blocks = 2 * seqs
    owners = min(8, seqs)
    peers = lax.axis_size("chan") // 2
    rows, width = features.shape[1:]
    bf16, f32 = jnp.bfloat16, jnp.float32
    vmem = pltpu.VMEM
    operands = (doc_lengths[None, :], features, short_weights, residues, rates, skip[None, :])
    wide = vmem((peers * rows * QUADS, LANES), f32)
    table = vmem((8 * MODES, LANES), f32)
    rim = vmem((2, width), bf16)
    moved = vmem((peers, rows, 2 * HALF), bf16)
    sent = vmem((peers, rows + EDGES, 2 * HALF), bf16)
    edges = vmem((peers, EDGES, 2 * HALF), bf16)
    edge = vmem((EDGES, 2 * HALF), bf16)
    height = MODES * QUADS // owners
    owned = vmem((owners, height, LANES), f32)
    dma = lambda *n: pltpu.SemaphoreType.DMA(n)
    return pl.pallas_call(
        kernel,
        out_shape=pltpu.VMEM((rows, width), bf16),
        in_specs=[pl.BlockSpec(memory_space=pl.ANY)] * 6,
        out_specs=VMEM,
        scratch_shapes=[vmem(x.shape, x.dtype) for x in operands]
        + [
            rim, rim,
            vmem((2, 2 * MODES + 8, HALF), f32),
            vmem((rows, width), bf16),
            sent, sent, edges, edge, edge, vmem((8 * QUADS * (peers + 1), LANES), f32),
            wide, wide, moved, moved,
            table, table, vmem((8, LANES), f32), table, table,
            owned, vmem((owners, height, LANES), bf16), vmem((blocks, height, LANES), bf16),
            vmem((blocks, height, LANES), f32), owned, owned,
            dma(7), dma(3), dma(5), pltpu.SemaphoreType.DMA, dma(peers), dma(peers), dma(peers), dma(peers), dma(peers),
            dma(blocks), dma(blocks), dma(owners), dma(owners),
        ],
        compiler_params=pltpu.CompilerParams(
            collective_id=0, has_side_effects=True, vmem_limit_bytes=58 * 2**20
        ),
    )(*operands)


def solution(mesh):
    placed = (P(None, ("seq", "chan"), None), P(), P(), P(None, "chan"), P(None, "chan"), P("chan"))
    return jax.shard_map(
        per_device, mesh=mesh, in_specs=placed, out_specs=P(("seq", "chan"), None), check_vma=False
    )
```
